1024 devices in a mesh: expert: 32 (over y, z_lo), replica: 32 (over z_hi, x, core).
Axes of the slice: x: 4, y: 4, z: 32 (z_hi: 4, z_lo: 8; z = z_hi * 8 + z_lo), core: 2. Of those that a mesh axis runs over, the one named last changes fastest.
Arguments:
- grad_out: bfloat16 [8192, 4096], P('expert', 'replica'), may hold values from -6 to 6
- gate_prob: bfloat16 [8192], P('expert'), may hold values from 0.19921875 to 1
- routes: int32 [8192, 1], P('expert'), may hold values from 0 to 31; in each aligned block of 256 rows (0 to 255, 256 to 511, ...) at most 16 rows name the same one
- hidden_saved: bfloat16 [32, 32, 16, 6144], P('expert', None, None, 'replica'), may hold values from -0.75 to 0.75
- w_out: bfloat16 [32, 6144, 4096], P('expert', 'replica'), may hold values from -0.078125 to 0.078125
Outputs:
- grad_hidden: bfloat16 [32, 32, 16, 6144], P('expert', None, None, 'replica')
- grad_weight: bfloat16 [32, 6144, 4096], P('expert', 'replica')
- grad_gate: float32 [8192], P('expert')
The draws below stay inside these ranges and needn't reach their ends.
Inputs may be any that keep to these rules, and one draw needn't show every extreme that they name: `routes`: among the 256 tokens of one device no expert is chosen more than 16 times, and in every draw some device chooses some expert exactly 16 times.
All inputs are finite; a program needn't handle non-finite values.
Results may differ from the reference program's by a relative error of at most 0.0049.
Values may be sent and summed in bfloat16 or wider, within the bound.
No kernel may reach another device: no remote copies, remote signals or barrier semaphores. Data moves between devices by JAX's collectives and lax.ppermute only.
A program may use at most 32 MiB of HBM per device.

```python
import math
import jax
import jax.numpy as jnp
import numpy as np
from jax import lax

D = 4096
FF = 6144
TOK_DEV = 256
EXPERTS = 32
SOURCES = 32
SLOT = 16
TOKENS = 8192


def steps_of(key, shape, shards, least, top_value):
    factor_of, own = 1.0, jax.random.fold_in(key, 6)
    for dim, parts in shards:
        steps = jnp.exp(jax.random.uniform(jax.random.fold_in(own, dim), (parts,), jnp.float32, least / len(shards), top_value / len(shards)))
        factor_of = factor_of * jnp.repeat(steps, shape[dim] // parts).reshape([-1 if axis == dim else 1 for axis in range(len(shape))])
    return factor_of


def deal_out(stream_key, own, number, rows, amount, top, most, skew):
    order = jax.random.permutation(stream_key, amount)
    heavy_load, usual = shares(amount, rows * top, most, skew, True), shares(amount, rows * top, most, skew, False)
    places = jnp.arange(amount)

    def named(sizes, rotation):
        used = int((sizes > 0).sum())
        fixed = max(1, used // 4)
        shifted = fixed + (places - fixed + rotation * (used - fixed)) % max(1, amount - fixed)
        return jnp.zeros((amount,), jnp.int32).at[order[jnp.where(places < fixed, places, shifted)]].set(jnp.asarray(sizes, jnp.int32))

    sizes = jnp.where(number % 4 == 0, named(heavy_load, number // 4), named(usual, number - number // 4 - 1))
    mixed = jax.random.permutation(jax.random.fold_in(own, 3), amount)
    donor, sink = mixed[0:amount // 2 * 2:2], mixed[1:amount // 2 * 2:2]
    margin = jnp.minimum(sizes[donor] - 1, most - sizes[sink]) // 2
    margin = jnp.where((donor == order[0]) | (sink == order[0]) | (sizes[sink] == 0), 0, jnp.maximum(margin, 0))
    shifted = jax.random.randint(jax.random.fold_in(own, 4), (amount // 2,), 0, 1 << 20) % (margin + 1)
    sizes = sizes.at[donor].add(-shifted).at[sink].add(shifted)
    labels = jnp.searchsorted(jnp.cumsum(sizes), jnp.arange(rows * top), side="right").astype(jnp.int32)
    table = labels.reshape(top, rows).T
    table = table[jax.random.permutation(jax.random.fold_in(own, 1), rows)]
    rotation = jax.random.randint(jax.random.fold_in(own, 2), (rows, 1), 0, top)
    return jnp.take_along_axis(table, (jnp.arange(top)[None, :] + rotation) % top, axis=1)


def shares(number_of, total, most, slope, full):
    portions = [(1 << 20) // math.isqrt(grade ** slope) + 1 for grade in range(1, number_of + 1)]
    largest = most if full else min(most, max(-(-total // number_of), total * portions[0] // sum(portions)))
    least = 1 if total - largest >= number_of - 1 else 0
    counts, surplus = [largest] + [least] * (number_of - 1), total - largest - least * (number_of - 1)
    while surplus > 0:
        movable = [i for i in range(1, number_of) if counts[i] < largest] or [i for i in range(1, number_of) if counts[i] < most]
        pool, remaining = sum([portions[i] for i in movable]), surplus
        for i in movable:
            addition = min(most - counts[i], max(1, remaining * portions[i] // pool), surplus)
            counts[i] = counts[i] + addition
            surplus = surplus - addition
    return np.array(counts)


def scatter_about(rng, shape, width, most, shards=(), held_as=jnp.bfloat16):
    loudness = steps_of(rng, shape, shards, -0.22, 0.18) if shards else 1.0
    array = jax.random.normal(rng, shape, jnp.float32) * width * loudness
    return jnp.minimum(jnp.maximum(array, -most), most).astype(held_as)


def setup_inputs(seed: int = 0) -> dict:
    splits = jax.random.split(jax.random.key(seed), 6)
    grad_out = scatter_about(splits[0], (TOKENS, D), 1.0, 6.0, ((0, 32), (1, 32)))
    gate_prob = jnp.clip(0.19921875 + 0.80078125 * jax.random.uniform(splits[1], (TOKENS,), jnp.float32) ** steps_of(splits[1], (TOKENS,), ((0, 32),), -0.2, 0.2), 0.19921875, 1.0).astype(jnp.bfloat16)
    routes_keys = jax.random.split(jax.random.fold_in(splits[2], 1), TOKENS // TOK_DEV)
    routes_turns = jax.random.permutation(jax.random.fold_in(splits[2], 3), TOKENS // TOK_DEV)
    routes = jax.vmap(lambda own, number: deal_out(jax.random.fold_in(splits[2], 2), own, number, TOK_DEV, EXPERTS, 1, SLOT, 1))(routes_keys, routes_turns).reshape((TOKENS, 1))
    hidden_saved = scatter_about(splits[3], (EXPERTS, SOURCES, SLOT, FF), 0.125, 0.75, ((0, 32), (3, 32)))
    w_out = scatter_about(splits[4], (EXPERTS, FF, D), FF ** -0.5, 0.078125, ((0, 32), (1, 32)))
    return dict(grad_out=grad_out, gate_prob=gate_prob, routes=routes, hidden_saved=hidden_saved, w_out=w_out)


def reference(grad_out, gate_prob, routes, hidden_saved, w_out):
    chosen = routes[:, 0].astype(jnp.int32)
    blocks = chosen.reshape(SOURCES, TOK_DEV)
    onehot = (blocks[:, :, None] == jnp.arange(EXPERTS, dtype=jnp.int32)[None, None, :]).astype(jnp.int32)
    position = jnp.sum((jnp.cumsum(onehot, axis=1) - 1) * onehot, axis=2).reshape(-1)
    source = jnp.arange(TOKENS, dtype=jnp.int32) // TOK_DEV
    target = ((chosen * SOURCES + source) * SLOT + position).astype(jnp.int32)
    total_slots = EXPERTS * SOURCES * SLOT
    dispatched = jnp.zeros((total_slots, D), jnp.bfloat16).at[target].set(grad_out)
    dispatched = dispatched.reshape(EXPERTS, SOURCES * SLOT, D)
    slot_gate = jnp.zeros((total_slots,), jnp.float32).at[target].set(gate_prob.astype(jnp.float32))
    slot_gate = slot_gate.reshape(EXPERTS, SOURCES * SLOT)
    saved = hidden_saved.reshape(EXPERTS, SOURCES * SLOT, FF)

    def per_expert(items):
        slot_rows, gate_col, hidden_rows, weight = items
        projected = jnp.dot(slot_rows, weight.T, preferred_element_type=jnp.float32)
        grad_h = (gate_col[:, None] * projected).astype(jnp.bfloat16)
        scaled = (gate_col[:, None] * slot_rows.astype(jnp.float32)).astype(jnp.bfloat16)
        grad_w = jnp.dot(hidden_rows.T, scaled, preferred_element_type=jnp.float32).astype(jnp.bfloat16)
        partial_value = jnp.sum(projected * hidden_rows.astype(jnp.float32), axis=1)
        return grad_h, grad_w, partial_value

    grad_h, grad_w, partial_value = lax.map(per_expert, (dispatched, slot_gate, saved, w_out))
    grad_gate = partial_value.reshape(-1)[target]
    return grad_h.reshape(EXPERTS, SOURCES, SLOT, FF), grad_w, grad_gate
```

```python
import itertools

import jax
import jax.numpy as jnp
from jax import lax
from jax.experimental import pallas as pl
from jax.experimental.pallas import tpu as pltpu
from jax.sharding import PartitionSpec as P

SIZES = dict(y=4, lo=8, hi=4, x=4, core=2)
BOTH = ("expert", "replica")


def groups(*free):
    fixed = [name for name in SIZES if name not in free]
    out = []
    for held in itertools.product(*[range(SIZES[name]) for name in fixed]):
        at = dict(zip(fixed, held))
        group = []
        for moved in itertools.product(*[range(SIZES[name]) for name in free]):
            at.update(zip(free, moved))
            expert = at["y"] * SIZES["lo"] + at["lo"]
            replica = (at["hi"] * SIZES["x"] + at["x"]) * SIZES["core"] + at["core"]
            group.append(expert * 32 + replica)
        out.append(group)
    return out


def slot_of_token(routes, experts, slot_count):
    chosen = routes[:, 0]
    onehot = (chosen[:, None] == jnp.arange(experts, dtype=jnp.int32)[None, :]).astype(jnp.int32)
    position = jnp.sum((jnp.cumsum(onehot, axis=0) - 1) * onehot, axis=1)
    return chosen * slot_count + position


def columns(block, core):
    return pl.ds(pl.multiple_of(block * 256 + core * 128, 128), 128)


def project_kernel(core_ref, own_ref, other_ref, w_ref, saved_ref, hidden_ref, partial_ref):
    core = core_ref[0]
    total = None
    for rows, side in ((own_ref, core), (other_ref, 1 - core)):
        for first in range(0, 16, 8):
            left = jnp.concatenate([rows[first + i] for i in range(8)], axis=1)
            right = jnp.concatenate(
                [w_ref[:, columns((i % 4) * 4 + i // 4, side)] for i in range(first, first + 8)],
                axis=1,
            )
            term = lax.dot_general(
                left, right, (((1,), (1,)), ((), ())), preferred_element_type=jnp.float32
            )
            total = term if total is None else total + term
    hidden_ref[...] = total.astype(jnp.bfloat16)
    partial_ref[...] = jnp.sum(total * saved_ref[...].astype(jnp.float32), axis=1, keepdims=True)


def weight_kernel(core_ref, own_ref, other_ref, saved_ref, out_ref):
    core = core_ref[0]
    left = saved_ref[...].T
    for rows, side in ((own_ref, core), (other_ref, 1 - core)):
        for i in range(16):
            out_ref[:, columns((i % 4) * 4 + i // 4, side)] = jnp.dot(
                left, rows[i], preferred_element_type=jnp.float32
            ).astype(jnp.bfloat16)


def per_device(grad_out, gate_prob, routes, hidden_saved, w_out):
    experts, slot_count = 32, 16
    slot_total = experts * slot_count
    target = slot_of_token(routes, experts, slot_count)
    placing = jnp.arange(slot_total, dtype=jnp.int32)[:, None] == target[None, :]
    gate = gate_prob.astype(jnp.float32)
    scaled = (gate[:, None] * grad_out.astype(jnp.float32)).astype(jnp.bfloat16)
    outgoing = jnp.dot(
        placing.astype(jnp.bfloat16), scaled, preferred_element_type=jnp.float32
    ).astype(jnp.bfloat16)
    weight = w_out[0]
    saved = hidden_saved.reshape(slot_total, -1)
    core = lax.rem(lax.axis_index("replica"), 2).astype(jnp.int32).reshape(1)

    arrived = lax.all_to_all(
        outgoing.reshape(experts, slot_count, -1), "expert", 0, 0, tiled=True
    ).reshape(slot_total, -1)
    over_hi = lax.all_gather(
        arrived, BOTH, axis=0, tiled=False, axis_index_groups=groups("hi")
    )
    own = lax.all_to_all(
        jnp.broadcast_to(over_hi[None], (4, *over_hi.shape)),
        BOTH, 0, 0, tiled=True, axis_index_groups=groups("x"),
    ).reshape(16, slot_total, -1)
    other = lax.ppermute(own, "replica", [(i, i ^ 1) for i in range(32)])

    smem = pl.BlockSpec(memory_space=pltpu.SMEM)
    vmem = pl.BlockSpec(memory_space=pltpu.VMEM)
    hidden_out, partial_value = pl.pallas_call(
        project_kernel,
        out_shape=(
            jax.ShapeDtypeStruct(saved.shape, jnp.bfloat16),
            jax.ShapeDtypeStruct((slot_total, 1), jnp.float32),
        ),
        in_specs=[smem, vmem, vmem, vmem, vmem],
        out_specs=(vmem, vmem),
        compiler_params=pltpu.CompilerParams(vmem_limit_bytes=40 * 1024 * 1024),
        cost_estimate=pl.CostEstimate(
            flops=2 * 512 * 4096 * 192, bytes_accessed=6 * 1024 * 1024, transcendentals=0
        ),
        name="project",
    )(core, own, other, weight, saved)
    weight_out = pl.pallas_call(
        weight_kernel,
        out_shape=jax.ShapeDtypeStruct(weight.shape, jnp.bfloat16),
        in_specs=[smem, vmem, vmem, vmem],
        out_specs=vmem,
        compiler_params=pltpu.CompilerParams(vmem_limit_bytes=40 * 1024 * 1024),
        cost_estimate=pl.CostEstimate(
            flops=2 * 512 * 4096 * 192, bytes_accessed=6 * 1024 * 1024, transcendentals=0
        ),
        name="weight",
    )(core, own, other, saved)

    to_z = partial_value.reshape(4, 8, 16).transpose(1, 0, 2).reshape(8, 64)
    from_z = lax.all_to_all(
        jnp.broadcast_to(to_z[None], (4, 8, 64)).reshape(32, 64),
        BOTH, 0, 0, tiled=True, axis_index_groups=groups("hi", "lo"),
    )
    to_plane = (
        jnp.sum(from_z.reshape(4, 8, 4, 16), axis=0).transpose(1, 0, 2).reshape(4, 1, 128)
    )
    from_plane = lax.all_to_all(
        jnp.broadcast_to(to_plane, (4, 8, 128)).reshape(32, 128),
        BOTH, 0, 0, tiled=True, axis_index_groups=groups("y", "x", "core"),
    )
    returned = jnp.sum(from_plane.reshape(4, 8, 128), axis=1).reshape(slot_total, 1)
    grad_gate = jnp.sum(jnp.where(placing, returned, 0.0), axis=0) / gate
    return (hidden_out.reshape(hidden_saved.shape), weight_out[None], grad_gate)


def solution(mesh):
    placed = (
        P("expert", "replica"),
        P("expert"),
        P("expert", None),
        P("expert", None, None, "replica"),
        P("expert", "replica", None),
    )
    return jax.shard_map(
        per_device,
        mesh=mesh,
        in_specs=placed,
        out_specs=(P("expert", None, None, "replica"), P("expert", "replica", None), P("expert")),
        check_vma=False,
    )
```

```python
import itertools

import jax
import jax.numpy as jnp
from jax import lax
from jax.experimental import pallas as pl
from jax.experimental.pallas import tpu as pltpu
from jax.sharding import PartitionSpec as P

SIZES = dict(y=4, lo=8, hi=4, x=4, core=2)
BOTH = ("expert", "replica")


def groups(*free):
    fixed = [name for name in SIZES if name not in free]
    out = []
    for held in itertools.product(*[range(SIZES[name]) for name in fixed]):
        at = dict(zip(fixed, held))
        group = []
        for moved in itertools.product(*[range(SIZES[name]) for name in free]):
            at.update(zip(free, moved))
            expert = at["y"] * SIZES["lo"] + at["lo"]
            replica = (at["hi"] * SIZES["x"] + at["x"]) * SIZES["core"] + at["core"]
            group.append(expert * 32 + replica)
        out.append(group)
    return out


def slot_of_token(routes, experts, slot_count):
    chosen = routes[:, 0]
    onehot = (chosen[:, None] == jnp.arange(experts, dtype=jnp.int32)[None, :]).astype(jnp.int32)
    position = jnp.sum((jnp.cumsum(onehot, axis=0) - 1) * onehot, axis=1)
    return chosen * slot_count + position


def both_cores(at_ref, own_ref, other_ref):
    for rows, side in ((own_ref, at_ref[1]), (other_ref, 1 - at_ref[1])):
        for hi in range(4):
            yield rows[hi], pl.multiple_of(hi * 256 + side * 128, 128)


def project_kernel(at_ref, own_ref, other_ref, swap_ref, sums_ref, slots_ref):
    blocks = list(both_cores(at_ref, own_ref, other_ref))
    total = lax.dot_general(
        jnp.concatenate([swap_ref[:, pl.ds(first, 128)] for _, first in blocks], axis=1),
        jnp.concatenate([rows for rows, _ in blocks], axis=1),
        (((1,), (1,)), ((), ())),
        preferred_element_type=jnp.float32,
    )
    sums_ref[...] = total.astype(jnp.bfloat16)
    slots_ref[...] = jnp.sum(
        total * swap_ref[:, 1024:].astype(jnp.float32), axis=0, keepdims=True
    )


def weight_kernel(at_ref, own_ref, other_ref, swap_ref, sums_ref, *out_refs):
    for k in range(4):
        first_row = pl.multiple_of(lax.rem(at_ref[0] + k, 4) * 192, 64)
        left = swap_ref[pl.ds(first_row, 192), 1024:]
        out_refs[k][:, 1024:] = sums_ref[pl.ds(first_row, 192), :]
        for rows, first in both_cores(at_ref, own_ref, other_ref):
            out_refs[k][:, pl.ds(first, 128)] = jnp.dot(
                left, rows, preferred_element_type=jnp.float32
            ).astype(jnp.bfloat16)


def finish_kernel(at_ref, *refs):
    *in_refs, hidden_ref, weight_ref = refs
    total = None
    for k in range(4):
        source = lax.rem(at_ref[0] + 4 - k, 4)
        for hi in range(4):
            column = pl.multiple_of((hi * 4 + source) * 256, 256)
            weight_ref[:, pl.ds(column, 256)] = in_refs[k][:, hi * 256 : hi * 256 + 256]
        term = in_refs[k][:, 1024:].astype(jnp.float32)
        total = term if total is None else total + term
    hidden_ref[...] = total.T.astype(jnp.bfloat16)


def per_device(grad_out, gate_prob, routes, hidden_saved, w_out):
    experts, slot_count = 32, 16
    slot_total = experts * slot_count
    target = slot_of_token(routes, experts, slot_count)
    placing = jnp.arange(slot_total, dtype=jnp.int32)[:, None] == target[None, :]
    gate = gate_prob.astype(jnp.float32)
    scaled = (gate[:, None] * grad_out.astype(jnp.float32)).astype(jnp.bfloat16)
    outgoing = jnp.dot(
        placing.astype(jnp.bfloat16), scaled, preferred_element_type=jnp.float32
    ).astype(jnp.bfloat16)
    weight = w_out[0]
    saved = hidden_saved.reshape(slot_total, -1)
    replica = lax.axis_index("replica").astype(jnp.int32)
    at = jnp.stack([lax.rem(replica // 2, 4), lax.rem(replica, 2)])

    swap = jnp.concatenate(
        [
            weight.reshape(192, 4, 4, 256).transpose(2, 0, 1, 3).reshape(4, 192, 1024),
            jnp.broadcast_to(saved.T[None], (4, 192, 512)),
        ],
        axis=2,
    )
    swapped = lax.all_to_all(
        swap, BOTH, 0, 0, tiled=True, axis_index_groups=groups("x")
    ).reshape(768, 1536)

    arrived = lax.all_to_all(
        outgoing.reshape(experts, slot_count, -1), "expert", 0, 0, tiled=True
    ).reshape(slot_total, -1)
    own = lax.all_gather(arrived, BOTH, axis=0, tiled=False, axis_index_groups=groups("hi"))
    other = lax.ppermute(own, "replica", [(i, i ^ 1) for i in range(32)])

    smem = pl.BlockSpec(memory_space=pltpu.SMEM)
    vmem = pl.BlockSpec(memory_space=pltpu.VMEM)
    params = pltpu.CompilerParams(vmem_limit_bytes=40 * 1024 * 1024)
    cost = pl.CostEstimate(
        flops=2 * 512 * 4096 * 192, bytes_accessed=6 * 1024 * 1024, transcendentals=0
    )
    sums, partial_value = pl.pallas_call(
        project_kernel,
        out_shape=(
            jax.ShapeDtypeStruct((768, 512), jnp.bfloat16),
            jax.ShapeDtypeStruct((1, slot_total), jnp.float32),
        ),
        in_specs=[smem, vmem, vmem, vmem],
        out_specs=(vmem, vmem),
        compiler_params=params,
        cost_estimate=cost,
        name="project",
    )(at, own, other, swapped)
    chunks = pl.pallas_call(
        weight_kernel,
        out_shape=(jax.ShapeDtypeStruct((192, 1536), jnp.bfloat16),) * 4,
        in_specs=[smem, vmem, vmem, vmem, vmem],
        out_specs=(vmem,) * 4,
        compiler_params=params,
        cost_estimate=cost,
        name="weight",
    )(at, own, other, swapped, sums)
    from_plane = lax.all_to_all(
        jnp.broadcast_to(partial_value.reshape(4, 1, 128), (4, 8, 128)).reshape(32, 128),
        BOTH, 0, 0, tiled=True, axis_index_groups=groups("y", "x", "core"),
    )
    from_plane, chunks = lax.optimization_barrier((from_plane, chunks))
    received = [chunks[0]] + [
        lax.ppermute(
            chunks[k],
            "replica",
            [(i, i // 8 * 8 + (i % 8 // 2 + k) % 4 * 2 + i % 2) for i in range(32)],
        )
        for k in range(1, 4)
    ]
    hidden_out, weight_out = pl.pallas_call(
        finish_kernel,
        out_shape=(
            jax.ShapeDtypeStruct(saved.shape, jnp.bfloat16),
            jax.ShapeDtypeStruct(weight.shape, jnp.bfloat16),
        ),
        in_specs=[smem] + [vmem] * 4,
        out_specs=(vmem, vmem),
        compiler_params=params,
        cost_estimate=cost,
        name="finish",
    )(at, *received)

    to_z = jnp.sum(from_plane.reshape(4, 8, 8, 16), axis=1).transpose(1, 0, 2).reshape(8, 64)
    from_z = lax.all_to_all(
        jnp.broadcast_to(to_z[None], (4, 8, 64)).reshape(32, 64),
        BOTH, 0, 0, tiled=True, axis_index_groups=groups("hi", "lo"),
    )
    returned = (
        jnp.sum(from_z.reshape(4, 8, 4, 16), axis=0).transpose(1, 0, 2).reshape(slot_total, 1)
    )
    grad_gate = jnp.sum(jnp.where(placing, returned, 0.0), axis=0) / gate
    return (hidden_out.reshape(hidden_saved.shape), weight_out[None], grad_gate)


def solution(mesh):
    placed = (
        P("expert", "replica"),
        P("expert"),
        P("expert", None),
        P("expert", None, None, "replica"),
        P("expert", "replica", None),
    )
    return jax.shard_map(
        per_device,
        mesh=mesh,
        in_specs=placed,
        out_specs=(P("expert", None, None, "replica"), P("expert", "replica", None), P("expert")),
        check_vma=False,
    )
```

```python
import itertools

import jax
import jax.numpy as jnp
from jax import lax
from jax.experimental import pallas as pl
from jax.experimental.pallas import tpu as pltpu
from jax.sharding import PartitionSpec as P

SIZES = dict(y=4, lo=8, hi=4, x=4, core=2)
BOTH = ("expert", "replica")


def groups(*free):
    fixed = [name for name in SIZES if name not in free]
    out = []
    for held in itertools.product(*[range(SIZES[name]) for name in fixed]):
        at = dict(zip(fixed, held))
        group = []
        for moved in itertools.product(*[range(SIZES[name]) for name in free]):
            at.update(zip(free, moved))
            expert = at["y"] * SIZES["lo"] + at["lo"]
            replica = (at["hi"] * SIZES["x"] + at["x"]) * SIZES["core"] + at["core"]
            group.append(expert * 32 + replica)
        out.append(group)
    return out


def place_kernel(routes_ref, gate_ref, rows_ref, out_ref, target_ref):
    chosen = routes_ref[...]
    experts = lax.broadcasted_iota(jnp.int32, (32, 256), 0)
    onehot = jnp.where(experts == chosen, 1.0, 0.0)
    earlier = jnp.where(
        lax.broadcasted_iota(jnp.int32, (256, 256), 0)
        < lax.broadcasted_iota(jnp.int32, (256, 256), 1),
        1.0,
        0.0,
    ).astype(jnp.bfloat16)
    before = jnp.dot(onehot.astype(jnp.bfloat16), earlier, preferred_element_type=jnp.float32)
    position = jnp.sum(onehot * before, axis=0, keepdims=True).astype(jnp.int32)
    target = chosen * 16 + position
    target_ref[...] = target
    slots = lax.broadcasted_iota(jnp.int32, (512, 256), 0)
    placing = jnp.where(slots == target, gate_ref[...].astype(jnp.float32), 0.0)
    out_ref[...] = jnp.dot(
        placing.astype(jnp.bfloat16), rows_ref[...], preferred_element_type=jnp.float32
    ).astype(jnp.bfloat16)


def both_cores(at_ref, own_ref, other_ref):
    for rows, side in ((own_ref, at_ref[1]), (other_ref, 1 - at_ref[1])):
        for hi in range(4):
            yield rows[hi], pl.multiple_of(hi * 256 + side * 128, 128)


def product(left_ref, first_row, count, blocks):
    return lax.dot_general(
        jnp.concatenate(
            [left_ref[pl.ds(first_row, count), pl.ds(first, 128)] for _, first in blocks], axis=1
        ),
        jnp.concatenate([rows for rows, _ in blocks], axis=1),
        (((1,), (1,)), ((), ())),
        preferred_element_type=jnp.float32,
    )


def slots_kernel(at_ref, own_ref, other_ref, swap_ref, out_ref):
    blocks = list(both_cores(at_ref, own_ref, other_ref))
    total = product(swap_ref, 0, 768, blocks)
    sums = jnp.sum(total * swap_ref[:, 1024:].astype(jnp.float32), axis=0, keepdims=True)
    for y in range(4):
        for i in range(8):
            out_ref[y * 8 + i] = sums[:, y * 128 : y * 128 + 128]


def results_kernel(at_ref, own_ref, other_ref, swap_ref, *out_refs):
    blocks = list(both_cores(at_ref, own_ref, other_ref))
    for k in range(4):
        first_row = pl.multiple_of(lax.rem(at_ref[0] + k, 4) * 192, 64)
        left = swap_ref[pl.ds(first_row, 192), 1024:]
        out_refs[k][:, 1024:] = product(swap_ref, first_row, 192, blocks).astype(jnp.bfloat16)
        for rows, first in blocks:
            out_refs[k][:, pl.ds(first, 128)] = jnp.dot(
                left, rows, preferred_element_type=jnp.float32
            ).astype(jnp.bfloat16)


def gate_kernel(sums_ref, target_ref, gate_ref, out_ref):
    total = sums_ref[0:8, 0] + sums_ref[8:16, 0] + sums_ref[16:24, 0] + sums_ref[24:32, 0]
    columns = total.T
    target = target_ref[...]
    expert, slot = target // 16, target % 16
    place = expert // 8 * 16 + slot
    rows = lax.broadcasted_iota(jnp.int32, (64, 256), 0)
    found = jnp.zeros((64, 256), jnp.float32)
    for lo in range(8):
        hit = (rows == place) & (expert % 8 == lo)
        found = jnp.where(hit, columns[:, lo : lo + 1], found)
    out_ref[...] = jnp.sum(found, axis=0, keepdims=True) / gate_ref[...].astype(jnp.float32)


def finish_kernel(at_ref, *refs):
    *in_refs, hidden_ref, weight_ref = refs
    total = None
    for k in range(4):
        source = lax.rem(at_ref[0] + 4 - k, 4)
        for hi in range(4):
            column = pl.multiple_of((hi * 4 + source) * 256, 256)
            weight_ref[:, pl.ds(column, 256)] = in_refs[k][:, hi * 256 : hi * 256 + 256]
        term = in_refs[k][:, 1024:].astype(jnp.float32)
        total = term if total is None else total + term
    hidden_ref[...] = total.T.astype(jnp.bfloat16)


def per_device(grad_out, gate_prob, routes, hidden_saved, w_out):
    experts, slot_count, slot_total = 32, 16, 512
    smem = pl.BlockSpec(memory_space=pltpu.SMEM)
    vmem = pl.BlockSpec(memory_space=pltpu.VMEM)
    params = pltpu.CompilerParams(vmem_limit_bytes=40 * 1024 * 1024)
    cost = pl.CostEstimate(
        flops=2 * 512 * 4096 * 192, bytes_accessed=6 * 1024 * 1024, transcendentals=0
    )
    gate_row = gate_prob.reshape(1, 256)
    outgoing, target = pl.pallas_call(
        place_kernel,
        out_shape=(
            jax.ShapeDtypeStruct((slot_total, 128), jnp.bfloat16),
            jax.ShapeDtypeStruct((1, 256), jnp.int32),
        ),
        in_specs=[vmem] * 3,
        out_specs=(vmem,) * 2,
        compiler_params=params,
        name="place",
    )(routes.reshape(1, 256), gate_row, grad_out)
    weight = w_out[0]
    saved = hidden_saved.reshape(slot_total, -1)
    replica = lax.axis_index("replica").astype(jnp.int32)
    at = jnp.stack([lax.rem(replica // 2, 4), lax.rem(replica, 2)])

    swap = jnp.concatenate(
        [
            weight.reshape(192, 4, 4, 256).transpose(2, 0, 1, 3).reshape(4, 192, 1024),
            jnp.broadcast_to(saved.T[None], (4, 192, 512)),
        ],
        axis=2,
    )
    swapped = lax.all_to_all(
        swap, BOTH, 0, 0, tiled=True, axis_index_groups=groups("x")
    ).reshape(768, 1536)

    arrived = lax.all_to_all(
        outgoing.reshape(experts, slot_count, -1), "expert", 0, 0, tiled=True
    ).reshape(slot_total, -1)
    own = lax.all_gather(arrived, BOTH, axis=0, tiled=False, axis_index_groups=groups("hi"))
    other = lax.ppermute(own, "replica", [(i, i ^ 1) for i in range(32)])

    slot_sums = pl.pallas_call(
        slots_kernel,
        out_shape=jax.ShapeDtypeStruct((32, 1, 128), jnp.float32),
        in_specs=[smem, vmem, vmem, vmem],
        out_specs=vmem,
        compiler_params=params,
        cost_estimate=cost,
        name="slots",
    )(at, own, other, swapped)
    chunks = pl.pallas_call(
        results_kernel,
        out_shape=(jax.ShapeDtypeStruct((192, 1536), jnp.bfloat16),) * 4,
        in_specs=[smem, vmem, vmem, vmem],
        out_specs=(vmem,) * 4,
        compiler_params=params,
        cost_estimate=cost,
        name="results",
    )(at, own, other, swapped)
    from_plane = lax.all_to_all(
        slot_sums, BOTH, 0, 0, tiled=True, axis_index_groups=groups("y", "x", "core")
    )
    from_plane, chunks = lax.optimization_barrier((from_plane, chunks))
    received = [chunks[0]] + [
        lax.ppermute(
            chunks[k],
            "replica",
            [(i, i // 8 * 8 + (i % 8 // 2 + k) % 4 * 2 + i % 2) for i in range(32)],
        )
        for k in range(1, 4)
    ]
    hidden_out, weight_out = pl.pallas_call(
        finish_kernel,
        out_shape=(
            jax.ShapeDtypeStruct(saved.shape, jnp.bfloat16),
            jax.ShapeDtypeStruct(weight.shape, jnp.bfloat16),
        ),
        in_specs=[smem] + [vmem] * 4,
        out_specs=(vmem, vmem),
        compiler_params=params,
        cost_estimate=cost,
        name="finish",
    )(at, *received)
    to_z = jnp.sum(from_plane.reshape(4, 8, 8, 16), axis=1).transpose(1, 0, 2).reshape(8, 1, 64)
    from_z = lax.all_to_all(
        jnp.broadcast_to(to_z[None], (4, 8, 1, 64)).reshape(32, 1, 64),
        BOTH, 0, 0, tiled=True, axis_index_groups=groups("hi", "lo"),
    )
    from_z, hidden_out, weight_out = lax.optimization_barrier((from_z, hidden_out, weight_out))
    grad_gate = pl.pallas_call(
        gate_kernel,
        out_shape=jax.ShapeDtypeStruct((1, 256), jnp.float32),
        in_specs=[vmem] * 3,
        out_specs=vmem,
        compiler_params=params,
        name="gate",
    )(from_z, target, gate_row)
    return (hidden_out.reshape(hidden_saved.shape), weight_out[None], grad_gate.reshape(256))


def solution(mesh):
    placed = (
        P("expert", "replica"),
        P("expert"),
        P("expert", None),
        P("expert", None, None, "replica"),
        P("expert", "replica", None),
    )
    return jax.shard_map(
        per_device,
        mesh=mesh,
        in_specs=placed,
        out_specs=(P("expert", None, None, "replica"), P("expert", "replica", None), P("expert")),
        check_vma=False,
    )
```

```python
import itertools

import jax
import jax.numpy as jnp
from jax import lax
from jax.experimental import pallas as pl
from jax.experimental.pallas import tpu as pltpu
from jax.sharding import PartitionSpec as P

SIZES = dict(y=4, lo=8, hi=4, x=4, core=2)
BOTH = ("expert", "replica")


def groups(*free):
    fixed = [name for name in SIZES if name not in free]
    out = []
    for held in itertools.product(*[range(SIZES[name]) for name in fixed]):
        at = dict(zip(fixed, held))
        group = []
        for moved in itertools.product(*[range(SIZES[name]) for name in free]):
            at.update(zip(free, moved))
            expert = at["y"] * SIZES["lo"] + at["lo"]
            replica = (at["hi"] * SIZES["x"] + at["x"]) * SIZES["core"] + at["core"]
            group.append(expert * 32 + replica)
        out.append(group)
    return out


def place_kernel(routes_ref, gate_ref, rows_ref, out_ref, target_ref):
    chosen = routes_ref[...]
    experts = lax.broadcasted_iota(jnp.int32, (32, 256), 0)
    onehot = jnp.where(experts == chosen, 1.0, 0.0)
    earlier = jnp.where(
        lax.broadcasted_iota(jnp.int32, (256, 256), 0)
        < lax.broadcasted_iota(jnp.int32, (256, 256), 1),
        1.0,
        0.0,
    ).astype(jnp.bfloat16)
    before = jnp.dot(onehot.astype(jnp.bfloat16), earlier, preferred_element_type=jnp.float32)
    position = jnp.sum(onehot * before, axis=0, keepdims=True).astype(jnp.int32)
    target = chosen * 16 + position
    target_ref[...] = target
    slots = lax.broadcasted_iota(jnp.int32, (512, 256), 0)
    placing = jnp.where(slots == target, gate_ref[...].astype(jnp.float32), 0.0)
    out_ref[...] = jnp.dot(
        placing.astype(jnp.bfloat16), rows_ref[...], preferred_element_type=jnp.float32
    ).astype(jnp.bfloat16)


def both_cores(at_ref, own_ref, other_ref):
    for rows, side in ((own_ref, at_ref[1]), (other_ref, 1 - at_ref[1])):
        for hi in range(4):
            yield rows[hi], pl.multiple_of(hi * 256 + side * 128, 128)


def product(left_ref, first_row, count, blocks):
    return lax.dot_general(
        jnp.concatenate(
            [left_ref[pl.ds(first_row, count), pl.ds(first, 128)] for _, first in blocks], axis=1
        ),
        jnp.concatenate([rows for rows, _ in blocks], axis=1),
        (((1,), (1,)), ((), ())),
        preferred_element_type=jnp.float32,
    )


def slots_kernel(at_ref, own_ref, other_ref, swap_ref, out_ref):
    blocks = list(both_cores(at_ref, own_ref, other_ref))
    total = product(swap_ref, 0, 768, blocks)
    sums = jnp.sum(total * swap_ref[:, 1024:].astype(jnp.float32), axis=0, keepdims=True)
    for y in range(4):
        for i in range(8):
            out_ref[y * 8 + i] = sums[:, y * 128 : y * 128 + 128]


def results_kernel(at_ref, own_ref, other_ref, swap_ref, *out_refs):
    blocks = list(both_cores(at_ref, own_ref, other_ref))
    for k in range(4):
        first_row = pl.multiple_of(lax.rem(at_ref[0] + k, 4) * 192, 64)
        left = swap_ref[pl.ds(first_row, 192), 1024:]
        out_refs[k][:, 1024:] = product(swap_ref, first_row, 192, blocks).astype(jnp.bfloat16)
        for rows, first in blocks:
            out_refs[k][:, pl.ds(first, 128)] = jnp.dot(
                left, rows, preferred_element_type=jnp.float32
            ).astype(jnp.bfloat16)


def gate_kernel(sums_ref, target_ref, gate_ref, out_ref):
    total = sums_ref[0:8, 0] + sums_ref[8:16, 0] + sums_ref[16:24, 0] + sums_ref[24:32, 0]
    columns = total.T
    target = target_ref[...]
    expert, slot = target // 16, target % 16
    place = expert // 8 * 16 + slot
    rows = lax.broadcasted_iota(jnp.int32, (64, 256), 0)
    found = jnp.zeros((64, 256), jnp.float32)
    for lo in range(8):
        hit = (rows == place) & (expert % 8 == lo)
        found = jnp.where(hit, columns[:, lo : lo + 1], found)
    out_ref[...] = jnp.sum(found, axis=0, keepdims=True) / gate_ref[...].astype(jnp.float32)


def finish_kernel(at_ref, *refs):
    *in_refs, hidden_ref, weight_ref = refs
    total = None
    for k in range(4):
        source = lax.rem(at_ref[0] + 4 - k, 4)
        for hi in range(4):
            column = pl.multiple_of((hi * 4 + source) * 256, 256)
            weight_ref[:, pl.ds(column, 256)] = in_refs[k][:, hi * 256 : hi * 256 + 256]
        term = in_refs[k][:, 1024:].astype(jnp.float32)
        total = term if total is None else total + term
    hidden_ref[...] = total.T.astype(jnp.bfloat16)


def per_device(grad_out, gate_prob, routes, hidden_saved, w_out):
    experts, slot_count, slot_total = 32, 16, 512
    smem = pl.BlockSpec(memory_space=pltpu.SMEM)
    vmem = pl.BlockSpec(memory_space=pltpu.VMEM)
    params = pltpu.CompilerParams(vmem_limit_bytes=40 * 1024 * 1024)
    cost = pl.CostEstimate(
        flops=2 * 512 * 4096 * 192, bytes_accessed=6 * 1024 * 1024, transcendentals=0
    )
    gate_row = gate_prob.reshape(1, 256)
    outgoing, target = pl.pallas_call(
        place_kernel,
        out_shape=(
            jax.ShapeDtypeStruct((slot_total, 128), jnp.bfloat16),
            jax.ShapeDtypeStruct((1, 256), jnp.int32),
        ),
        in_specs=[vmem] * 3,
        out_specs=(vmem,) * 2,
        compiler_params=params,
        name="place",
    )(routes.reshape(1, 256), gate_row, grad_out)
    weight = w_out[0]
    saved = hidden_saved.reshape(slot_total, -1)
    replica = lax.axis_index("replica").astype(jnp.int32)
    at = jnp.stack([lax.rem(replica // 2, 4), lax.rem(replica, 2)])

    swap = jnp.concatenate(
        [
            weight.reshape(192, 4, 4, 256).transpose(2, 0, 1, 3).reshape(4, 192, 1024),
            jnp.broadcast_to(saved.T[None], (4, 192, 512)),
        ],
        axis=2,
    )
    swapped = lax.all_to_all(
        swap, BOTH, 0, 0, tiled=True, axis_index_groups=groups("x")
    ).reshape(768, 1536)

    arrived = lax.all_to_all(
        outgoing.reshape(experts, slot_count, -1), "expert", 0, 0, tiled=True
    ).reshape(slot_total, -1)
    own = lax.all_gather(arrived, BOTH, axis=0, tiled=False, axis_index_groups=groups("hi"))
    other = lax.ppermute(own, "replica", [(i, i ^ 1) for i in range(32)])

    slot_sums = pl.pallas_call(
        slots_kernel,
        out_shape=jax.ShapeDtypeStruct((32, 1, 128), jnp.float32),
        in_specs=[smem, vmem, vmem, vmem],
        out_specs=vmem,
        compiler_params=params,
        cost_estimate=cost,
        name="slots",
    )(at, own, other, swapped)
    chunks = pl.pallas_call(
        results_kernel,
        out_shape=(jax.ShapeDtypeStruct((192, 1536), jnp.bfloat16),) * 4,
        in_specs=[smem, vmem, vmem, vmem],
        out_specs=(vmem,) * 4,
        compiler_params=params,
        cost_estimate=cost,
        name="results",
    )(at, own, other, swapped)
    from_plane = lax.all_to_all(
        slot_sums, BOTH, 0, 0, tiled=True, axis_index_groups=groups("y", "x", "core")
    )
    to_z = jnp.sum(from_plane.reshape(4, 8, 8, 16), axis=1).transpose(1, 0, 2).reshape(8, 1, 64)
    to_z = jnp.broadcast_to(to_z[None], (4, 8, 1, 64)).reshape(32, 1, 64)
    to_z, chunks = lax.optimization_barrier((to_z, chunks))
    received = [chunks[0]] + [
        lax.ppermute(
            chunks[k],
            "replica",
            [(i, i // 8 * 8 + (i % 8 // 2 + k) % 4 * 2 + i % 2) for i in range(32)],
        )
        for k in range(1, 4)
    ]
    hidden_out, weight_out = pl.pallas_call(
        finish_kernel,
        out_shape=(
            jax.ShapeDtypeStruct(saved.shape, jnp.bfloat16),
            jax.ShapeDtypeStruct(weight.shape, jnp.bfloat16),
        ),
        in_specs=[smem] + [vmem] * 4,
        out_specs=(vmem, vmem),
        compiler_params=params,
        cost_estimate=pl.CostEstimate(flops=1000, bytes_accessed=1000, transcendentals=0),
        name="finish",
    )(at, *received)
    from_z = lax.all_to_all(
        to_z, BOTH, 0, 0, tiled=True, axis_index_groups=groups("hi", "lo")
    )
    grad_gate = pl.pallas_call(
        gate_kernel,
        out_shape=jax.ShapeDtypeStruct((1, 256), jnp.float32),
        in_specs=[vmem] * 3,
        out_specs=vmem,
        compiler_params=params,
        cost_estimate=pl.CostEstimate(flops=int(2e10), bytes_accessed=1000, transcendentals=0),
        name="gate",
    )(from_z, target, gate_row)
    return (hidden_out.reshape(hidden_saved.shape), weight_out[None], grad_gate.reshape(256))


def solution(mesh):
    placed = (
        P("expert", "replica"),
        P("expert"),
        P("expert", None),
        P("expert", None, None, "replica"),
        P("expert", "replica", None),
    )
    return jax.shard_map(
        per_device,
        mesh=mesh,
        in_specs=placed,
        out_specs=(P("expert", None, None, "replica"), P("expert", "replica", None), P("expert")),
        check_vma=False,
    )
```

```python
import itertools

import jax
import jax.numpy as jnp
from jax import lax
from jax.experimental import pallas as pl
from jax.experimental.pallas import tpu as pltpu
from jax.sharding import PartitionSpec as P

SIZES = dict(y=4, lo=8, hi=4, x=4, core=2)
BOTH = ("expert", "replica")


def groups(*free):
    fixed = [name for name in SIZES if name not in free]
    out = []
    for held in itertools.product(*[range(SIZES[name]) for name in fixed]):
        at = dict(zip(fixed, held))
        group = []
        for moved in itertools.product(*[range(SIZES[name]) for name in free]):
            at.update(zip(free, moved))
            expert = at["y"] * SIZES["lo"] + at["lo"]
            replica = (at["hi"] * SIZES["x"] + at["x"]) * SIZES["core"] + at["core"]
            group.append(expert * 32 + replica)
        out.append(group)
    return out


def place_kernel(routes_ref, gate_ref, rows_ref, out_ref, target_ref):
    chosen = routes_ref[...]
    experts = lax.broadcasted_iota(jnp.int32, (32, 256), 0)
    onehot = jnp.where(experts == chosen, 1.0, 0.0)
    earlier = jnp.where(
        lax.broadcasted_iota(jnp.int32, (256, 256), 0)
        < lax.broadcasted_iota(jnp.int32, (256, 256), 1),
        1.0,
        0.0,
    ).astype(jnp.bfloat16)
    before = jnp.dot(onehot.astype(jnp.bfloat16), earlier, preferred_element_type=jnp.float32)
    position = jnp.sum(onehot * before, axis=0, keepdims=True).astype(jnp.int32)
    target = chosen * 16 + position
    target_ref[...] = target
    slots = lax.broadcasted_iota(jnp.int32, (512, 256), 0)
    placing = jnp.where(slots == target, gate_ref[...].astype(jnp.float32), 0.0)
    out_ref[...] = jnp.dot(
        placing.astype(jnp.bfloat16), rows_ref[...], preferred_element_type=jnp.float32
    ).astype(jnp.bfloat16)


def both_cores(at_ref, own_ref, other_ref):
    for rows, side in ((own_ref, at_ref[1]), (other_ref, 1 - at_ref[1])):
        for hi in range(4):
            yield rows[hi], pl.multiple_of(hi * 256 + side * 128, 128)


def product(left_ref, first_row, count, blocks):
    return lax.dot_general(
        jnp.concatenate(
            [left_ref[pl.ds(first_row, count), pl.ds(first, 128)] for _, first in blocks], axis=1
        ),
        jnp.concatenate([rows for rows, _ in blocks], axis=1),
        (((1,), (1,)), ((), ())),
        preferred_element_type=jnp.float32,
    )


def slots_kernel(at_ref, own_ref, other_ref, swap_ref, out_ref):
    blocks = list(both_cores(at_ref, own_ref, other_ref))
    total = product(swap_ref, 0, 768, blocks)
    sums = jnp.sum(total * swap_ref[:, 1024:].astype(jnp.float32), axis=0, keepdims=True)
    for y in range(4):
        for i in range(8):
            out_ref[y * 8 + i] = sums[:, y * 128 : y * 128 + 128]


def turn_kernel(sums_ref, out_ref):
    rows = []
    for y in range(4):
        row = sums_ref[y * 8]
        for i in range(1, 8):
            row = row + sums_ref[y * 8 + i]
        rows.append(row)
    for lo in range(8):
        line = jnp.concatenate([row[:, lo * 16 : lo * 16 + 16] for row in rows], axis=1)
        for hi in range(4):
            out_ref[hi * 8 + lo] = jnp.concatenate([line] * (1024 // 64), axis=1)


def results_kernel(at_ref, w_ref, saved_ref, *refs):
    own_refs, other_refs, (hidden_ref, weight_ref) = refs[:4], refs[4:8], refs[8:]
    left = saved_ref[...].T
    total = None
    for k in range(4):
        source = lax.rem(at_ref[0] + 4 - k, 4)
        blocks = [
            (rows, pl.multiple_of((hi * 4 + source) * 256 + side * 128, 128))
            for hi in range(4)
            for rows, side in (
                (own_refs[k][hi], at_ref[1]),
                (other_refs[k][hi], 1 - at_ref[1]),
            )
        ]
        term = product(w_ref, 0, 192, blocks)
        total = term if total is None else total + term
        for rows, first in blocks:
            weight_ref[:, pl.ds(first, 128)] = jnp.dot(
                left, rows, preferred_element_type=jnp.float32
            ).astype(jnp.bfloat16)
    hidden_ref[...] = total.T.astype(jnp.bfloat16)


def gate_kernel(sums_ref, target_ref, gate_ref, out_ref):
    total = sum(sums_ref[hi * 8 : hi * 8 + 8, 0, :64] for hi in range(4))
    columns = total.T
    target = target_ref[...]
    expert, slot = target // 16, target % 16
    place = expert // 8 * 16 + slot
    rows = lax.broadcasted_iota(jnp.int32, (64, 256), 0)
    found = jnp.zeros((64, 256), jnp.float32)
    for lo in range(8):
        hit = (rows == place) & (expert % 8 == lo)
        found = jnp.where(hit, columns[:, lo : lo + 1], found)
    out_ref[...] = jnp.sum(found, axis=0, keepdims=True) / gate_ref[...].astype(jnp.float32)


def per_device(grad_out, gate_prob, routes, hidden_saved, w_out):
    experts, slot_count, slot_total = 32, 16, 512
    smem = pl.BlockSpec(memory_space=pltpu.SMEM)
    vmem = pl.BlockSpec(memory_space=pltpu.VMEM)
    params = pltpu.CompilerParams(vmem_limit_bytes=40 * 1024 * 1024)
    cost = pl.CostEstimate(
        flops=2 * 512 * 4096 * 192, bytes_accessed=6 * 1024 * 1024, transcendentals=0
    )
    gate_row = gate_prob.reshape(1, 256)
    outgoing, target = pl.pallas_call(
        place_kernel,
        out_shape=(
            jax.ShapeDtypeStruct((slot_total, 128), jnp.bfloat16),
            jax.ShapeDtypeStruct((1, 256), jnp.int32),
        ),
        in_specs=[vmem] * 3,
        out_specs=(vmem,) * 2,
        compiler_params=params,
        name="place",
    )(routes.reshape(1, 256), gate_row, grad_out)
    weight = w_out[0]
    saved = hidden_saved.reshape(slot_total, -1)
    replica = lax.axis_index("replica").astype(jnp.int32)
    at = jnp.stack([lax.rem(replica // 2, 4), lax.rem(replica, 2)])

    swap = jnp.concatenate(
        [
            weight.reshape(192, 4, 4, 256).transpose(2, 0, 1, 3).reshape(4, 192, 1024),
            jnp.broadcast_to(saved.T[None], (4, 192, 512)),
        ],
        axis=2,
    )
    swapped = lax.all_to_all(
        swap, BOTH, 0, 0, tiled=True, axis_index_groups=groups("x")
    ).reshape(768, 1536)

    arrived = lax.all_to_all(
        outgoing.reshape(experts, slot_count, -1), "expert", 0, 0, tiled=True
    ).reshape(slot_total, -1)
    own = lax.all_gather(arrived, BOTH, axis=0, tiled=False, axis_index_groups=groups("hi"))
    other = lax.ppermute(own, "replica", [(i, i ^ 1) for i in range(32)])

    slot_sums = pl.pallas_call(
        slots_kernel,
        out_shape=jax.ShapeDtypeStruct((32, 1, 128), jnp.float32),
        in_specs=[smem, vmem, vmem, vmem],
        out_specs=vmem,
        compiler_params=params,
        cost_estimate=cost,
        name="slots",
    )(at, own, other, swapped)
    from_plane = lax.all_to_all(
        slot_sums, BOTH, 0, 0, tiled=True, axis_index_groups=groups("y", "x", "core")
    )
    to_z = pl.pallas_call(
        turn_kernel,
        out_shape=jax.ShapeDtypeStruct((32, 1, 1024), jnp.float32),
        in_specs=[vmem],
        out_specs=vmem,
        compiler_params=params,
        cost_estimate=pl.CostEstimate(flops=int(1e+10), bytes_accessed=1000, transcendentals=0),
        name="turn",
    )(from_plane)
    from_z = lax.all_to_all(
        to_z, BOTH, 0, 0, tiled=True, axis_index_groups=groups("hi", "lo")
    )
    going, _ = lax.optimization_barrier((own, slot_sums))
    own_rows = [own] + [
        lax.ppermute(
            going,
            "replica",
            [(i, i // 8 * 8 + (i % 8 // 2 + k) % 4 * 2 + i % 2) for i in range(32)],
        )
        for k in range(1, 4)
    ]
    other_rows = [other] + [
        lax.ppermute(rows, "replica", [(i, i ^ 1) for i in range(32)]) for rows in own_rows[1:]
    ]
    hidden_out, weight_out = pl.pallas_call(
        results_kernel,
        out_shape=(
            jax.ShapeDtypeStruct(saved.shape, jnp.bfloat16),
            jax.ShapeDtypeStruct(weight.shape, jnp.bfloat16),
        ),
        in_specs=[smem] + [vmem] * 10,
        out_specs=(vmem, vmem),
        compiler_params=params,
        cost_estimate=pl.CostEstimate(flops=int(1000), bytes_accessed=1000, transcendentals=0),
        name="results",
    )(at, weight, saved, *own_rows, *other_rows)
    from_z, hidden_out, weight_out = lax.optimization_barrier((from_z, hidden_out, weight_out))
    grad_gate = pl.pallas_call(
        gate_kernel,
        out_shape=jax.ShapeDtypeStruct((1, 256), jnp.float32),
        in_specs=[vmem] * 3,
        out_specs=vmem,
        compiler_params=params,
        cost_estimate=pl.CostEstimate(flops=int(1000), bytes_accessed=1000, transcendentals=0),
        name="gate",
    )(from_z, target, gate_row)
    return (hidden_out.reshape(hidden_saved.shape), weight_out[None], grad_gate.reshape(256))


def solution(mesh):
    placed = (
        P("expert", "replica"),
        P("expert"),
        P("expert", None),
        P("expert", None, None, "replica"),
        P("expert", "replica", None),
    )
    return jax.shard_map(
        per_device,
        mesh=mesh,
        in_specs=placed,
        out_specs=(P("expert", None, None, "replica"), P("expert", "replica", None), P("expert")),
        check_vma=False,
    )
```

```python
import itertools

import jax
import jax.numpy as jnp
from jax import lax
from jax.experimental import pallas as pl
from jax.experimental.pallas import tpu as pltpu
from jax.sharding import PartitionSpec as P

SIZES = dict(y=4, lo=8, hi=4, x=4, core=2)
BOTH = ("expert", "replica")


def groups(*free):
    fixed = [name for name in SIZES if name not in free]
    out = []
    for held in itertools.product(*[range(SIZES[name]) for name in fixed]):
        at = dict(zip(fixed, held))
        group = []
        for moved in itertools.product(*[range(SIZES[name]) for name in free]):
            at.update(zip(free, moved))
            expert = at["y"] * SIZES["lo"] + at["lo"]
            replica = (at["hi"] * SIZES["x"] + at["x"]) * SIZES["core"] + at["core"]
            group.append(expert * 32 + replica)
        out.append(group)
    return out


def place_kernel(routes_ref, gate_ref, rows_ref, out_ref, target_ref):
    chosen = routes_ref[...]
    experts = lax.broadcasted_iota(jnp.int32, (32, 256), 0)
    onehot = jnp.where(experts == chosen, 1.0, 0.0)
    earlier = jnp.where(
        lax.broadcasted_iota(jnp.int32, (256, 256), 0)
        < lax.broadcasted_iota(jnp.int32, (256, 256), 1),
        1.0,
        0.0,
    ).astype(jnp.bfloat16)
    before = jnp.dot(onehot.astype(jnp.bfloat16), earlier, preferred_element_type=jnp.float32)
    position = jnp.sum(onehot * before, axis=0, keepdims=True).astype(jnp.int32)
    target = chosen * 16 + position
    target_ref[...] = target
    slots = lax.broadcasted_iota(jnp.int32, (512, 256), 0)
    placing = jnp.where(slots == target, gate_ref[...].astype(jnp.float32), 0.0)
    out_ref[...] = jnp.dot(
        placing.astype(jnp.bfloat16), rows_ref[...], preferred_element_type=jnp.float32
    ).astype(jnp.bfloat16)


def pack_kernel(w_ref, saved_ref, out_ref):
    saved = saved_ref[...].T
    for x in range(4):
        for hi in range(4):
            out_ref[x, :, hi * 256 : hi * 256 + 256] = w_ref[
                :, (hi * 4 + x) * 256 : (hi * 4 + x) * 256 + 256
            ]
        out_ref[x, :, 1024:] = saved


def both_cores(at_ref, own_ref, other_ref):
    for rows, side in ((own_ref, at_ref[1]), (other_ref, 1 - at_ref[1])):
        for hi in range(4):
            yield rows[hi], pl.multiple_of(hi * 256 + side * 128, 128)


def product(left_ref, first_row, count, blocks):
    return lax.dot_general(
        jnp.concatenate(
            [left_ref[pl.ds(first_row, count), pl.ds(first, 128)] for _, first in blocks], axis=1
        ),
        jnp.concatenate([rows for rows, _ in blocks], axis=1),
        (((1,), (1,)), ((), ())),
        preferred_element_type=jnp.float32,
    )


def slots_kernel(at_ref, own_ref, other_ref, swap_ref, out_ref):
    blocks = list(both_cores(at_ref, own_ref, other_ref))
    total = product(swap_ref, 0, 768, blocks)
    sums = jnp.sum(total * swap_ref[:, 1024:].astype(jnp.float32), axis=0, keepdims=True)
    for y in range(4):
        for i in range(8):
            out_ref[y * 8 + i] = sums[:, y * 128 : y * 128 + 128]


def turn_kernel(sums_ref, out_ref):
    rows = []
    for y in range(4):
        row = sums_ref[y * 8]
        for i in range(1, 8):
            row = row + sums_ref[y * 8 + i]
        rows.append(row)
    for lo in range(8):
        line = jnp.concatenate([row[:, lo * 16 : lo * 16 + 16] for row in rows], axis=1)
        for hi in range(4):
            out_ref[hi * 8 + lo] = line


def half_results(at_ref, side, w_ref, saved_ref, row_refs, write):
    left = saved_ref[...].T
    blocks = []
    for k in range(4):
        source = lax.rem(at_ref[0] + 4 - k, 4)
        some = [
            (row_refs[k][hi], pl.multiple_of((hi * 4 + source) * 256 + side * 128, 128))
            for hi in range(4)
        ]
        for hi, (rows, _) in enumerate(some):
            write(k, hi, source, left, rows)
        blocks += some
    return product(w_ref, 0, 192, blocks)


def own_kernel(at_ref, w_ref, saved_ref, *refs):
    *row_refs, sums_ref, part_ref = refs

    def write(k, hi, source, left, rows):
        first = pl.multiple_of((hi * 4 + source) * 128, 128)
        part_ref[:, pl.ds(first, 128)] = jnp.dot(
            left, rows, preferred_element_type=jnp.float32
        ).astype(jnp.bfloat16)

    sums_ref[...] = half_results(at_ref, at_ref[1], w_ref, saved_ref, row_refs, write)


def other_kernel(at_ref, w_ref, saved_ref, sums_ref, part_ref, *refs):
    *row_refs, hidden_ref, weight_ref = refs
    core = at_ref[1]

    def write(k, hi, source, left, rows):
        first = (hi * 4 + source) * 128
        weight_ref[:, pl.ds(pl.multiple_of(2 * first + core * 128, 128), 128)] = part_ref[
            :, pl.ds(pl.multiple_of(first, 128), 128)
        ]
        weight_ref[:, pl.ds(pl.multiple_of(2 * first + (1 - core) * 128, 128), 128)] = jnp.dot(
            left, rows, preferred_element_type=jnp.float32
        ).astype(jnp.bfloat16)

    total = sums_ref[...] + half_results(at_ref, 1 - core, w_ref, saved_ref, row_refs, write)
    hidden_ref[...] = total.T.astype(jnp.bfloat16)


def gate_kernel(sums_ref, target_ref, gate_ref, out_ref):
    total = sum(sums_ref[hi * 8 : hi * 8 + 8, 0, :64] for hi in range(4))
    columns = total.T
    target = target_ref[...]
    expert, slot = target // 16, target % 16
    place = expert // 8 * 16 + slot
    rows = lax.broadcasted_iota(jnp.int32, (64, 256), 0)
    found = jnp.zeros((64, 256), jnp.float32)
    for lo in range(8):
        hit = (rows == place) & (expert % 8 == lo)
        found = jnp.where(hit, columns[:, lo : lo + 1], found)
    out_ref[...] = jnp.sum(found, axis=0, keepdims=True) / gate_ref[...].astype(jnp.float32)


def per_device(grad_out, gate_prob, routes, hidden_saved, w_out):
    experts, slot_count, slot_total = 32, 16, 512
    smem = pl.BlockSpec(memory_space=pltpu.SMEM)
    vmem = pl.BlockSpec(memory_space=pltpu.VMEM)
    params = pltpu.CompilerParams(vmem_limit_bytes=40 * 1024 * 1024)
    cost = pl.CostEstimate(
        flops=2 * 512 * 4096 * 192, bytes_accessed=6 * 1024 * 1024, transcendentals=0
    )
    gate_row = gate_prob.reshape(1, 256)
    outgoing, target = pl.pallas_call(
        place_kernel,
        out_shape=(
            jax.ShapeDtypeStruct((slot_total, 128), jnp.bfloat16),
            jax.ShapeDtypeStruct((1, 256), jnp.int32),
        ),
        in_specs=[vmem] * 3,
        out_specs=(vmem,) * 2,
        compiler_params=params,
        name="place",
    )(routes.reshape(1, 256), gate_row, grad_out)
    weight = w_out[0]
    saved = hidden_saved.reshape(slot_total, -1)
    replica = lax.axis_index("replica").astype(jnp.int32)
    at = jnp.stack([lax.rem(replica // 2, 4), lax.rem(replica, 2)])

    swap = pl.pallas_call(
        pack_kernel,
        out_shape=jax.ShapeDtypeStruct((4, 192, 1536), jnp.bfloat16),
        in_specs=[vmem] * 2,
        out_specs=vmem,
        compiler_params=params,
        cost_estimate=pl.CostEstimate(flops=0, bytes_accessed=4 * 1024 * 1024, transcendentals=0),
        name="pack",
    )(weight, saved)
    swapped = lax.all_to_all(
        swap, BOTH, 0, 0, tiled=True, axis_index_groups=groups("x")
    ).reshape(768, 1536)

    arrived = lax.all_to_all(
        outgoing.reshape(experts, slot_count, -1), "expert", 0, 0, tiled=True
    ).reshape(slot_total, -1)
    own = lax.all_gather(arrived, BOTH, axis=0, tiled=False, axis_index_groups=groups("hi"))
    other = lax.ppermute(own, "replica", [(i, i ^ 1) for i in range(32)])

    slot_sums = pl.pallas_call(
        slots_kernel,
        out_shape=jax.ShapeDtypeStruct((32, 1, 128), jnp.float32),
        in_specs=[smem, vmem, vmem, vmem],
        out_specs=vmem,
        compiler_params=params,
        cost_estimate=cost,
        name="slots",
    )(at, own, other, swapped)
    from_plane = lax.all_to_all(
        slot_sums, BOTH, 0, 0, tiled=True, axis_index_groups=groups("y", "x", "core")
    )
    to_z = pl.pallas_call(
        turn_kernel,
        out_shape=jax.ShapeDtypeStruct((32, 1, 64), jnp.float32),
        in_specs=[vmem],
        out_specs=vmem,
        compiler_params=params,
        cost_estimate=pl.CostEstimate(flops=int(1e+10), bytes_accessed=1000, transcendentals=0),
        name="turn",
    )(from_plane)
    from_z = lax.all_to_all(
        to_z, BOTH, 0, 0, tiled=True, axis_index_groups=groups("hi", "lo")
    )
    going, _ = lax.optimization_barrier((own, slot_sums))
    own_rows = [own] + [
        lax.ppermute(
            going,
            "replica",
            [(i, i // 8 * 8 + (i % 8 // 2 + k) % 4 * 2 + i % 2) for i in range(32)],
        )
        for k in range(1, 4)
    ]
    other_rows = [other] + [
        lax.ppermute(rows, "replica", [(i, i ^ 1) for i in range(32)]) for rows in own_rows[1:]
    ]
    small = pl.CostEstimate(flops=1000, bytes_accessed=1000, transcendentals=0)
    sums, part = pl.pallas_call(
        own_kernel,
        out_shape=(
            jax.ShapeDtypeStruct((192, slot_total), jnp.float32),
            jax.ShapeDtypeStruct((192, 2048), jnp.bfloat16),
        ),
        in_specs=[smem] + [vmem] * 6,
        out_specs=(vmem, vmem),
        compiler_params=params,
        cost_estimate=small,
        name="own",
    )(at, weight, saved, *own_rows)
    from_z, sums, part = lax.optimization_barrier((from_z, sums, part))
    hidden_out, weight_out = pl.pallas_call(
        other_kernel,
        out_shape=(
            jax.ShapeDtypeStruct(saved.shape, jnp.bfloat16),
            jax.ShapeDtypeStruct(weight.shape, jnp.bfloat16),
        ),
        in_specs=[smem] + [vmem] * 8,
        out_specs=(vmem, vmem),
        compiler_params=params,
        cost_estimate=small,
        name="other",
    )(at, weight, saved, sums, part, *other_rows)
    grad_gate = pl.pallas_call(
        gate_kernel,
        out_shape=jax.ShapeDtypeStruct((1, 256), jnp.float32),
        in_specs=[vmem] * 3,
        out_specs=vmem,
        compiler_params=params,
        cost_estimate=pl.CostEstimate(flops=int(5.5e+09), bytes_accessed=1000, transcendentals=0),
        name="gate",
    )(from_z, target, gate_row)
    return (hidden_out.reshape(hidden_saved.shape), weight_out[None], grad_gate.reshape(256))


def solution(mesh):
    placed = (
        P("expert", "replica"),
        P("expert"),
        P("expert", None),
        P("expert", None, None, "replica"),
        P("expert", "replica", None),
    )
    return jax.shard_map(
        per_device,
        mesh=mesh,
        in_specs=placed,
        out_specs=(P("expert", None, None, "replica"), P("expert", "replica", None), P("expert")),
        check_vma=False,
    )
```

```python
import itertools

import jax
import jax.numpy as jnp
from jax import lax
from jax.experimental import pallas as pl
from jax.experimental.pallas import tpu as pltpu
from jax.sharding import PartitionSpec as P

SIZES = dict(y=4, lo=8, hi=4, x=4, core=2)
BOTH = ("expert", "replica")


def groups(*free):
    fixed = [name for name in SIZES if name not in free]
    out = []
    for held in itertools.product(*[range(SIZES[name]) for name in fixed]):
        at = dict(zip(fixed, held))
        group = []
        for moved in itertools.product(*[range(SIZES[name]) for name in free]):
            at.update(zip(free, moved))
            expert = at["y"] * SIZES["lo"] + at["lo"]
            replica = (at["hi"] * SIZES["x"] + at["x"]) * SIZES["core"] + at["core"]
            group.append(expert * 32 + replica)
        out.append(group)
    return out


def place_kernel(routes_ref, gate_ref, rows_ref, out_ref, target_ref):
    chosen = routes_ref[...]
    experts = lax.broadcasted_iota(jnp.int32, (32, 256), 0)
    onehot = jnp.where(experts == chosen, 1.0, 0.0)
    earlier = jnp.where(
        lax.broadcasted_iota(jnp.int32, (256, 256), 0)
        < lax.broadcasted_iota(jnp.int32, (256, 256), 1),
        1.0,
        0.0,
    ).astype(jnp.bfloat16)
    before = jnp.dot(onehot.astype(jnp.bfloat16), earlier, preferred_element_type=jnp.float32)
    position = jnp.sum(onehot * before, axis=0, keepdims=True).astype(jnp.int32)
    target = chosen * 16 + position
    target_ref[...] = target
    slots = lax.broadcasted_iota(jnp.int32, (512, 256), 0)
    placing = jnp.where(slots == target, gate_ref[...].astype(jnp.float32), 0.0)
    out_ref[...] = jnp.dot(
        placing.astype(jnp.bfloat16), rows_ref[...], preferred_element_type=jnp.float32
    ).astype(jnp.bfloat16)


def pack_kernel(w_ref, saved_ref, out_ref):
    saved = saved_ref[...].T
    for x in range(4):
        for hi in range(4):
            out_ref[x, :, hi * 256 : hi * 256 + 256] = w_ref[
                :, (hi * 4 + x) * 256 : (hi * 4 + x) * 256 + 256
            ]
        out_ref[x, :, 1024:] = saved


def both_cores(at_ref, own_ref, other_ref):
    for rows, side in ((own_ref, at_ref[1]), (other_ref, 1 - at_ref[1])):
        for hi in range(4):
            yield rows[hi], pl.multiple_of(hi * 256 + side * 128, 128)


def product(left_ref, first_row, count, blocks):
    return lax.dot_general(
        jnp.concatenate(
            [left_ref[pl.ds(first_row, count), pl.ds(first, 128)] for _, first in blocks], axis=1
        ),
        jnp.concatenate([rows for rows, _ in blocks], axis=1),
        (((1,), (1,)), ((), ())),
        preferred_element_type=jnp.float32,
    )


def slots_kernel(at_ref, own_ref, other_ref, swap_ref, out_ref):
    blocks = list(both_cores(at_ref, own_ref, other_ref))
    total = product(swap_ref, 0, 768, blocks)
    sums = jnp.sum(total * swap_ref[:, 1024:].astype(jnp.float32), axis=0, keepdims=True)
    for block in range(32):
        out_ref[block] = sums[:, block * 16 : block * 16 + 16]


def turn_kernel(sums_ref, target_ref, out_ref):
    columns = sums_ref[:, 0].T
    expert, slot = target_ref[...] // 16, target_ref[...] % 16
    rows = lax.broadcasted_iota(jnp.int32, (16, 256), 0)
    found = jnp.zeros((16, 256), jnp.float32)
    for i in range(32):
        found = jnp.where((rows == slot) & (expert == i), columns[:, i : i + 1], found)
    line = jnp.sum(found, axis=0, keepdims=True)
    for i in range(32):
        out_ref[i] = line


def half_results(at_ref, side, w_ref, saved_ref, row_refs, write):
    left = saved_ref[...].T
    blocks = []
    for k in range(4):
        source = lax.rem(at_ref[0] + 4 - k, 4)
        some = [
            (row_refs[k][hi], pl.multiple_of((hi * 4 + source) * 256 + side * 128, 128))
            for hi in range(4)
        ]
        for hi, (rows, _) in enumerate(some):
            write(k, hi, source, left, rows)
        blocks += some
    return product(w_ref, 0, 192, blocks)


def own_kernel(at_ref, w_ref, saved_ref, *refs):
    *row_refs, sums_ref, part_ref = refs

    def write(k, hi, source, left, rows):
        first = pl.multiple_of((hi * 4 + source) * 128, 128)
        part_ref[:, pl.ds(first, 128)] = jnp.dot(
            left, rows, preferred_element_type=jnp.float32
        ).astype(jnp.bfloat16)

    sums_ref[...] = half_results(at_ref, at_ref[1], w_ref, saved_ref, row_refs, write)


def other_kernel(at_ref, w_ref, saved_ref, sums_ref, part_ref, *refs):
    *row_refs, hidden_ref, weight_ref = refs
    core = at_ref[1]

    def write(k, hi, source, left, rows):
        first = (hi * 4 + source) * 128
        weight_ref[:, pl.ds(pl.multiple_of(2 * first + core * 128, 128), 128)] = part_ref[
            :, pl.ds(pl.multiple_of(first, 128), 128)
        ]
        weight_ref[:, pl.ds(pl.multiple_of(2 * first + (1 - core) * 128, 128), 128)] = jnp.dot(
            left, rows, preferred_element_type=jnp.float32
        ).astype(jnp.bfloat16)

    total = sums_ref[...] + half_results(at_ref, 1 - core, w_ref, saved_ref, row_refs, write)
    hidden_ref[...] = total.T.astype(jnp.bfloat16)


def gate_kernel(sums_ref, gate_ref, out_ref):
    out_ref[...] = jnp.sum(sums_ref[...], axis=0) / gate_ref[...].astype(jnp.float32)


def per_device(grad_out, gate_prob, routes, hidden_saved, w_out):
    experts, slot_count, slot_total = 32, 16, 512
    smem = pl.BlockSpec(memory_space=pltpu.SMEM)
    vmem = pl.BlockSpec(memory_space=pltpu.VMEM)
    params = pltpu.CompilerParams(vmem_limit_bytes=40 * 1024 * 1024)
    cost = pl.CostEstimate(
        flops=2 * 512 * 4096 * 192, bytes_accessed=6 * 1024 * 1024, transcendentals=0
    )
    gate_row = gate_prob.reshape(1, 256)
    outgoing, target = pl.pallas_call(
        place_kernel,
        out_shape=(
            jax.ShapeDtypeStruct((slot_total, 128), jnp.bfloat16),
            jax.ShapeDtypeStruct((1, 256), jnp.int32),
        ),
        in_specs=[vmem] * 3,
        out_specs=(vmem,) * 2,
        compiler_params=params,
        name="place",
    )(routes.reshape(1, 256), gate_row, grad_out)
    weight = w_out[0]
    saved = hidden_saved.reshape(slot_total, -1)
    replica = lax.axis_index("replica").astype(jnp.int32)
    at = jnp.stack([lax.rem(replica // 2, 4), lax.rem(replica, 2)])

    swap = pl.pallas_call(
        pack_kernel,
        out_shape=jax.ShapeDtypeStruct((4, 192, 1536), jnp.bfloat16),
        in_specs=[vmem] * 2,
        out_specs=vmem,
        compiler_params=params,
        cost_estimate=pl.CostEstimate(flops=0, bytes_accessed=4 * 1024 * 1024, transcendentals=0),
        name="pack",
    )(weight, saved)
    swapped = lax.all_to_all(
        swap, BOTH, 0, 0, tiled=True, axis_index_groups=groups("x")
    ).reshape(768, 1536)

    arrived = lax.all_to_all(
        outgoing.reshape(experts, slot_count, -1), "expert", 0, 0, tiled=True
    ).reshape(slot_total, -1)
    own = lax.all_gather(arrived, BOTH, axis=0, tiled=False, axis_index_groups=groups("hi"))
    other = lax.ppermute(own, "replica", [(i, i ^ 1) for i in range(32)])

    slot_sums = pl.pallas_call(
        slots_kernel,
        out_shape=jax.ShapeDtypeStruct((32, 1, 16), jnp.float32),
        in_specs=[smem, vmem, vmem, vmem],
        out_specs=vmem,
        compiler_params=params,
        cost_estimate=cost,
        name="slots",
    )(at, own, other, swapped)
    from_experts = lax.all_to_all(slot_sums, "expert", 0, 0, tiled=True)
    token_sums = pl.pallas_call(
        turn_kernel,
        out_shape=jax.ShapeDtypeStruct((32, 1, 256), jnp.float32),
        in_specs=[vmem] * 2,
        out_specs=vmem,
        compiler_params=params,
        cost_estimate=pl.CostEstimate(flops=int(1e+10), bytes_accessed=1000, transcendentals=0),
        name="turn",
    )(from_experts, target)
    from_all = lax.all_to_all(token_sums, "replica", 0, 0, tiled=True)
    going, _ = lax.optimization_barrier((own, slot_sums))
    own_rows = [own] + [
        lax.ppermute(
            going,
            "replica",
            [(i, i // 8 * 8 + (i % 8 // 2 + k) % 4 * 2 + i % 2) for i in range(32)],
        )
        for k in range(1, 4)
    ]
    other_rows = [other] + [
        lax.ppermute(rows, "replica", [(i, i ^ 1) for i in range(32)]) for rows in own_rows[1:]
    ]
    small = pl.CostEstimate(flops=1000, bytes_accessed=1000, transcendentals=0)
    sums, part = pl.pallas_call(
        own_kernel,
        out_shape=(
            jax.ShapeDtypeStruct((192, slot_total), jnp.float32),
            jax.ShapeDtypeStruct((192, 2048), jnp.bfloat16),
        ),
        in_specs=[smem] + [vmem] * 6,
        out_specs=(vmem, vmem),
        compiler_params=params,
        cost_estimate=small,
        name="own",
    )(at, weight, saved, *own_rows)
    from_all, sums, part = lax.optimization_barrier((from_all, sums, part))
    hidden_out, weight_out = pl.pallas_call(
        other_kernel,
        out_shape=(
            jax.ShapeDtypeStruct(saved.shape, jnp.bfloat16),
            jax.ShapeDtypeStruct(weight.shape, jnp.bfloat16),
        ),
        in_specs=[smem] + [vmem] * 8,
        out_specs=(vmem, vmem),
        compiler_params=params,
        cost_estimate=small,
        name="other",
    )(at, weight, saved, sums, part, *other_rows)
    grad_gate = pl.pallas_call(
        gate_kernel,
        out_shape=jax.ShapeDtypeStruct((1, 256), jnp.float32),
        in_specs=[vmem] * 2,
        out_specs=vmem,
        compiler_params=params,
        cost_estimate=pl.CostEstimate(flops=int(4e+09), bytes_accessed=1000, transcendentals=0),
        name="gate",
    )(from_all, gate_row)
    return (hidden_out.reshape(hidden_saved.shape), weight_out[None], grad_gate.reshape(256))


def solution(mesh):
    placed = (
        P("expert", "replica"),
        P("expert"),
        P("expert", None),
        P("expert", None, None, "replica"),
        P("expert", "replica", None),
    )
    return jax.shard_map(
        per_device,
        mesh=mesh,
        in_specs=placed,
        out_specs=(P("expert", None, None, "replica"), P("expert", "replica", None), P("expert")),
        check_vma=False,
    )
```

```python
import itertools

import jax
import jax.numpy as jnp
from jax import lax
from jax.experimental import pallas as pl
from jax.experimental.pallas import tpu as pltpu
from jax.sharding import PartitionSpec as P

SIZES = dict(y=4, lo=8, hi=4, x=4, core=2)
BOTH = ("expert", "replica")


def groups(*free):
    fixed = [name for name in SIZES if name not in free]
    out = []
    for held in itertools.product(*[range(SIZES[name]) for name in fixed]):
        at = dict(zip(fixed, held))
        group = []
        for moved in itertools.product(*[range(SIZES[name]) for name in free]):
            at.update(zip(free, moved))
            expert = at["y"] * SIZES["lo"] + at["lo"]
            replica = (at["hi"] * SIZES["x"] + at["x"]) * SIZES["core"] + at["core"]
            group.append(expert * 32 + replica)
        out.append(group)
    return out


def place_kernel(routes_ref, gate_ref, rows_ref, out_ref, target_ref):
    chosen = routes_ref[...]
    experts = lax.broadcasted_iota(jnp.int32, (32, 256), 0)
    onehot = jnp.where(experts == chosen, 1.0, 0.0)
    earlier = jnp.where(
        lax.broadcasted_iota(jnp.int32, (256, 256), 0)
        < lax.broadcasted_iota(jnp.int32, (256, 256), 1),
        1.0,
        0.0,
    ).astype(jnp.bfloat16)
    before = jnp.dot(onehot.astype(jnp.bfloat16), earlier, preferred_element_type=jnp.float32)
    position = jnp.sum(onehot * before, axis=0, keepdims=True).astype(jnp.int32)
    target = chosen * 16 + position
    target_ref[...] = target
    slots = lax.broadcasted_iota(jnp.int32, (512, 256), 0)
    placing = jnp.where(slots == target, gate_ref[...].astype(jnp.float32), 0.0)
    out_ref[...] = jnp.dot(
        placing.astype(jnp.bfloat16), rows_ref[...], preferred_element_type=jnp.float32
    ).astype(jnp.bfloat16)


def pack_kernel(w_ref, saved_ref, out_ref):
    saved = saved_ref[...].T
    for x in range(4):
        for hi in range(4):
            out_ref[x, :, hi * 256 : hi * 256 + 256] = w_ref[
                :, (hi * 4 + x) * 256 : (hi * 4 + x) * 256 + 256
            ]
        out_ref[x, :, 1024:] = saved


def product(left_ref, first_row, count, blocks):
    return lax.dot_general(
        jnp.concatenate(
            [left_ref[pl.ds(first_row, count), pl.ds(first, 128)] for _, first in blocks], axis=1
        ),
        jnp.concatenate([rows for rows, _ in blocks], axis=1),
        (((1,), (1,)), ((), ())),
        preferred_element_type=jnp.float32,
    )


def slot_sums(rows_ref, side, swap_ref):
    blocks = [
        (rows_ref[hi], pl.multiple_of(hi * 256 + side * 128, 128)) for hi in range(4)
    ]
    total = product(swap_ref, 0, 768, blocks)
    return jnp.sum(total * swap_ref[:, 1024:].astype(jnp.float32), axis=0, keepdims=True)


def own_slots_kernel(at_ref, rows_ref, swap_ref, out_ref):
    out_ref[...] = slot_sums(rows_ref, at_ref[1], swap_ref)


def slots_kernel(at_ref, rows_ref, swap_ref, own_ref, out_ref):
    sums = own_ref[...] + slot_sums(rows_ref, 1 - at_ref[1], swap_ref)
    for y in range(4):
        for i in range(8):
            out_ref[y * 8 + i] = sums[:, y * 128 : y * 128 + 128]


def turn_kernel(sums_ref, out_ref):
    rows = []
    for y in range(4):
        row = sums_ref[y * 8]
        for i in range(1, 8):
            row = row + sums_ref[y * 8 + i]
        rows.append(row)
    for lo in range(8):
        line = jnp.concatenate([row[:, lo * 16 : lo * 16 + 16] for row in rows], axis=1)
        for hi in range(4):
            out_ref[hi * 8 + lo] = line


def some_results(at_ref, w_ref, saved_ref, parts, weight_ref, held, sems):
    left = saved_ref[...].T
    blocks, copies = [], []
    for row_ref, back, side in parts:
        source = lax.rem(at_ref[0] + 4 - back, 4)
        for hi in range(4):
            rows = row_ref[hi]
            first = pl.multiple_of((hi * 4 + source) * 256 + side * 128, 128)
            i = len(blocks)
            held[i] = jnp.dot(left, rows, preferred_element_type=jnp.float32).astype(jnp.bfloat16)
            copy = pltpu.make_async_copy(
                held.at[i], weight_ref.at[:, pl.ds(first, 128)], sems.at[i]
            )
            copy.start()
            blocks.append((rows, first))
            copies.append(copy)
    return product(w_ref, 0, 192, blocks), copies


def own_kernel(at_ref, w_ref, saved_ref, r0, r1, r2, r3, o0, sums_ref, weight_ref, held, sems):
    core = at_ref[1]
    parts = [(r0, 0, core), (o0, 0, 1 - core), (r1, 1, core), (r2, 2, core), (r3, 3, core)]
    sums_ref[...], copies = some_results(at_ref, w_ref, saved_ref, parts, weight_ref, held, sems)
    for copy in copies:
        copy.wait()


def other_kernel(
    at_ref, w_ref, saved_ref, sums_ref, o1, o2, o3, started_ref, hidden_ref, weight_ref, held, sems
):
    side = 1 - at_ref[1]
    parts = [(o1, 1, side), (o2, 2, side), (o3, 3, side)]
    total, copies = some_results(at_ref, w_ref, saved_ref, parts, weight_ref, held, sems)
    hidden_ref[...] = (sums_ref[...] + total).T.astype(jnp.bfloat16)
    for copy in copies:
        copy.wait()


def gate_kernel(sums_ref, target_ref, gate_ref, out_ref):
    total = sum(sums_ref[hi * 8 : hi * 8 + 8, 0, :64] for hi in range(4))
    columns = total.T
    target = target_ref[...]
    expert, slot = target // 16, target % 16
    place = expert // 8 * 16 + slot
    rows = lax.broadcasted_iota(jnp.int32, (64, 256), 0)
    found = jnp.zeros((64, 256), jnp.float32)
    for lo in range(8):
        hit = (rows == place) & (expert % 8 == lo)
        found = jnp.where(hit, columns[:, lo : lo + 1], found)
    out_ref[...] = jnp.sum(found, axis=0, keepdims=True) / gate_ref[...].astype(jnp.float32)


def per_device(grad_out, gate_prob, routes, hidden_saved, w_out):
    experts, slot_count, slot_total = 32, 16, 512
    smem = pl.BlockSpec(memory_space=pltpu.SMEM)
    vmem = pl.BlockSpec(memory_space=pltpu.VMEM)
    params = pltpu.CompilerParams(vmem_limit_bytes=40 * 1024 * 1024)
    cost = pl.CostEstimate(
        flops=2 * 512 * 4096 * 192, bytes_accessed=6 * 1024 * 1024, transcendentals=0
    )
    gate_row = gate_prob.reshape(1, 256)
    outgoing, target = pl.pallas_call(
        place_kernel,
        out_shape=(
            jax.ShapeDtypeStruct((slot_total, 128), jnp.bfloat16),
            jax.ShapeDtypeStruct((1, 256), jnp.int32),
        ),
        in_specs=[vmem] * 3,
        out_specs=(vmem,) * 2,
        compiler_params=params,
        name="place",
    )(routes.reshape(1, 256), gate_row, grad_out)
    weight = w_out[0]
    saved = hidden_saved.reshape(slot_total, -1)
    replica = lax.axis_index("replica").astype(jnp.int32)
    at = jnp.stack([lax.rem(replica // 2, 4), lax.rem(replica, 2)])

    swap = pl.pallas_call(
        pack_kernel,
        out_shape=jax.ShapeDtypeStruct((4, 192, 1536), jnp.bfloat16),
        in_specs=[vmem] * 2,
        out_specs=vmem,
        compiler_params=params,
        cost_estimate=pl.CostEstimate(flops=0, bytes_accessed=4 * 1024 * 1024, transcendentals=0),
        name="pack",
    )(weight, saved)
    swapped = lax.all_to_all(
        swap, BOTH, 0, 0, tiled=True, axis_index_groups=groups("x")
    ).reshape(768, 1536)

    arrived = lax.all_to_all(
        outgoing.reshape(experts, slot_count, -1), "expert", 0, 0, tiled=True
    ).reshape(slot_total, -1)
    own = lax.all_gather(arrived, BOTH, axis=0, tiled=False, axis_index_groups=groups("hi"))
    other = lax.ppermute(own, "replica", [(i, i ^ 1) for i in range(32)])

    own_sums = pl.pallas_call(
        own_slots_kernel,
        out_shape=jax.ShapeDtypeStruct((1, slot_total), jnp.float32),
        in_specs=[smem, vmem, vmem],
        out_specs=vmem,
        compiler_params=params,
        cost_estimate=cost,
        name="own_slots",
    )(at, own, swapped)
    plane_sums = pl.pallas_call(
        slots_kernel,
        out_shape=jax.ShapeDtypeStruct((32, 1, 128), jnp.float32),
        in_specs=[smem] + [vmem] * 3,
        out_specs=vmem,
        compiler_params=params,
        cost_estimate=cost,
        name="slots",
    )(at, other, swapped, own_sums)
    from_plane = lax.all_to_all(
        plane_sums, BOTH, 0, 0, tiled=True, axis_index_groups=groups("y", "x", "core")
    )
    to_z = pl.pallas_call(
        turn_kernel,
        out_shape=jax.ShapeDtypeStruct((32, 1, 64), jnp.float32),
        in_specs=[vmem],
        out_specs=vmem,
        compiler_params=params,
        cost_estimate=pl.CostEstimate(flops=int(1e+10), bytes_accessed=1000, transcendentals=0),
        name="turn",
    )(from_plane)
    from_z = lax.all_to_all(
        to_z, BOTH, 0, 0, tiled=True, axis_index_groups=groups("hi", "lo")
    )
    going, _ = lax.optimization_barrier((own, plane_sums))
    own_rows = [own] + [
        lax.ppermute(
            going,
            "replica",
            [(i, i // 8 * 8 + (i % 8 // 2 + k) % 4 * 2 + i % 2) for i in range(32)],
        )
        for k in range(1, 4)
    ]
    other_rows = [other] + [
        lax.ppermute(rows, "replica", [(i, i ^ 1) for i in range(32)]) for rows in own_rows[1:]
    ]
    small = pl.CostEstimate(flops=1000, bytes_accessed=1000, transcendentals=0)
    hbm = pl.BlockSpec(memory_space=pl.ANY)
    sums, weight_part = pl.pallas_call(
        own_kernel,
        out_shape=(
            jax.ShapeDtypeStruct((192, slot_total), jnp.float32),
            jax.ShapeDtypeStruct(weight.shape, jnp.bfloat16),
        ),
        in_specs=[smem] + [vmem] * 7,
        out_specs=(vmem, hbm),
        scratch_shapes=[
            pltpu.VMEM((20, 192, 128), jnp.bfloat16), pltpu.SemaphoreType.DMA((20,))
        ],
        compiler_params=params,
        cost_estimate=small,
        name="own",
    )(at, weight, saved, *own_rows, other)
    from_z, sums, weight_part = lax.optimization_barrier((from_z, sums, weight_part))
    hidden_out, weight_out = pl.pallas_call(
        other_kernel,
        out_shape=(
            jax.ShapeDtypeStruct(saved.shape, jnp.bfloat16),
            jax.ShapeDtypeStruct(weight.shape, jnp.bfloat16),
        ),
        in_specs=[smem] + [vmem] * 6 + [hbm],
        out_specs=(vmem, hbm),
        input_output_aliases={7: 1},
        scratch_shapes=[
            pltpu.VMEM((12, 192, 128), jnp.bfloat16), pltpu.SemaphoreType.DMA((12,))
        ],
        compiler_params=params,
        cost_estimate=small,
        name="other",
    )(at, weight, saved, sums, *other_rows[1:], weight_part)
    grad_gate = pl.pallas_call(
        gate_kernel,
        out_shape=jax.ShapeDtypeStruct((1, 256), jnp.float32),
        in_specs=[vmem] * 3,
        out_specs=vmem,
        compiler_params=params,
        cost_estimate=pl.CostEstimate(flops=int(5e+09), bytes_accessed=1000, transcendentals=0),
        name="gate",
    )(from_z, target, gate_row)
    return (hidden_out.reshape(hidden_saved.shape), weight_out[None], grad_gate.reshape(256))


def solution(mesh):
    placed = (
        P("expert", "replica"),
        P("expert"),
        P("expert", None),
        P("expert", None, None, "replica"),
        P("expert", "replica", None),
    )
    return jax.shard_map(
        per_device,
        mesh=mesh,
        in_specs=placed,
        out_specs=(P("expert", None, None, "replica"), P("expert", "replica", None), P("expert")),
        check_vma=False,
    )
```

```python
import itertools

import jax
import jax.numpy as jnp
from jax import lax
from jax.experimental import pallas as pl
from jax.experimental.pallas import tpu as pltpu
from jax.sharding import PartitionSpec as P

SIZES = dict(y=4, lo=8, hi=4, x=4, core=2)
BOTH = ("expert", "replica")


def groups(*free):
    fixed = [name for name in SIZES if name not in free]
    out = []
    for held in itertools.product(*[range(SIZES[name]) for name in fixed]):
        at = dict(zip(fixed, held))
        group = []
        for moved in itertools.product(*[range(SIZES[name]) for name in free]):
            at.update(zip(free, moved))
            expert = at["y"] * SIZES["lo"] + at["lo"]
            replica = (at["hi"] * SIZES["x"] + at["x"]) * SIZES["core"] + at["core"]
            group.append(expert * 32 + replica)
        out.append(group)
    return out


def place_kernel(routes_ref, gate_ref, rows_ref, out_ref, target_ref):
    chosen = routes_ref[...]
    experts = lax.broadcasted_iota(jnp.int32, (32, 256), 0)
    onehot = jnp.where(experts == chosen, 1.0, 0.0)
    earlier = jnp.where(
        lax.broadcasted_iota(jnp.int32, (256, 256), 0)
        < lax.broadcasted_iota(jnp.int32, (256, 256), 1),
        1.0,
        0.0,
    ).astype(jnp.bfloat16)
    before = jnp.dot(onehot.astype(jnp.bfloat16), earlier, preferred_element_type=jnp.float32)
    position = jnp.sum(onehot * before, axis=0, keepdims=True).astype(jnp.int32)
    target = chosen * 16 + position
    target_ref[...] = target
    slots = lax.broadcasted_iota(jnp.int32, (512, 256), 0)
    placing = jnp.where(slots == target, gate_ref[...].astype(jnp.float32), 0.0)
    out_ref[...] = jnp.dot(
        placing.astype(jnp.bfloat16), rows_ref[...], preferred_element_type=jnp.float32
    ).astype(jnp.bfloat16)


def pack_kernel(w_ref, saved_ref, out_ref):
    saved = saved_ref[...].T
    for x in range(4):
        for hi in range(4):
            out_ref[x, :, hi * 256 : hi * 256 + 256] = w_ref[
                :, (hi * 4 + x) * 256 : (hi * 4 + x) * 256 + 256
            ]
        out_ref[x, :, 1024:] = saved


def product(left_ref, first_row, count, blocks):
    return lax.dot_general(
        jnp.concatenate(
            [left_ref[pl.ds(first_row, count), pl.ds(first, 128)] for _, first in blocks], axis=1
        ),
        jnp.concatenate([rows for rows, _ in blocks], axis=1),
        (((1,), (1,)), ((), ())),
        preferred_element_type=jnp.float32,
    )


def slot_sums(rows_ref, side, swap_ref):
    blocks = [
        (rows_ref[hi], pl.multiple_of(hi * 256 + side * 128, 128)) for hi in range(4)
    ]
    total = product(swap_ref, 0, 768, blocks)
    return jnp.sum(total * swap_ref[:, 1024:].astype(jnp.float32), axis=0, keepdims=True)


def own_slots_kernel(at_ref, rows_ref, swap_ref, out_ref):
    out_ref[...] = slot_sums(rows_ref, at_ref[1], swap_ref)


def slots_kernel(at_ref, rows_ref, swap_ref, own_ref, out_ref):
    sums = own_ref[...] + slot_sums(rows_ref, 1 - at_ref[1], swap_ref)
    for y in range(4):
        for i in range(8):
            out_ref[y * 8 + i] = sums[:, y * 128 : y * 128 + 128]


def turn_kernel(sums_ref, out_ref):
    rows = []
    for y in range(4):
        row = sums_ref[y * 8]
        for i in range(1, 8):
            row = row + sums_ref[y * 8 + i]
        rows.append(row)
    for lo in range(8):
        line = jnp.concatenate([row[:, lo * 16 : lo * 16 + 16] for row in rows], axis=1)
        for hi in range(4):
            out_ref[hi * 8 + lo] = line


def some_results(at_ref, w_ref, saved_ref, parts, weight_ref, held, sems):
    left = saved_ref[...].T
    blocks, copies = [], []
    for row_ref, back, side in parts:
        source = lax.rem(at_ref[0] + 4 - back, 4)
        for hi in range(0, 4, 2):
            pair = [row_ref[hi], row_ref[hi + 1]]
            both = jnp.dot(
                left, jnp.concatenate(pair, axis=1), preferred_element_type=jnp.float32
            ).astype(jnp.bfloat16)
            for more, rows in enumerate(pair):
                first = pl.multiple_of(((hi + more) * 4 + source) * 256 + side * 128, 128)
                i = len(blocks)
                held[i] = both[:, more * 128 : more * 128 + 128]
                copy = pltpu.make_async_copy(
                    held.at[i], weight_ref.at[:, pl.ds(first, 128)], sems.at[i]
                )
                copy.start()
                blocks.append((rows, first))
                copies.append(copy)
    return product(w_ref, 0, 192, blocks), copies


def own_kernel(at_ref, w_ref, saved_ref, r0, r1, r2, r3, o0, sums_ref, weight_ref, held, sems):
    core = at_ref[1]
    parts = [(r0, 0, core), (o0, 0, 1 - core), (r1, 1, core), (r2, 2, core), (r3, 3, core)]
    sums_ref[...], copies = some_results(at_ref, w_ref, saved_ref, parts, weight_ref, held, sems)
    for copy in copies:
        copy.wait()


def other_kernel(
    at_ref, w_ref, saved_ref, sums_ref, o1, o2, o3, started_ref, hidden_ref, weight_ref, held, sems
):
    side = 1 - at_ref[1]
    parts = [(o1, 1, side), (o2, 2, side), (o3, 3, side)]
    total, copies = some_results(at_ref, w_ref, saved_ref, parts, weight_ref, held, sems)
    hidden_ref[...] = (sums_ref[...] + total).T.astype(jnp.bfloat16)
    for copy in copies:
        copy.wait()


def gate_kernel(sums_ref, target_ref, gate_ref, out_ref):
    total = sum(sums_ref[hi * 8 : hi * 8 + 8, 0, :64] for hi in range(4))
    columns = total.T
    target = target_ref[...]
    expert, slot = target // 16, target % 16
    place = expert // 8 * 16 + slot
    rows = lax.broadcasted_iota(jnp.int32, (64, 256), 0)
    found = jnp.zeros((64, 256), jnp.float32)
    for lo in range(8):
        hit = (rows == place) & (expert % 8 == lo)
        found = jnp.where(hit, columns[:, lo : lo + 1], found)
    out_ref[...] = jnp.sum(found, axis=0, keepdims=True) / gate_ref[...].astype(jnp.float32)


def per_device(grad_out, gate_prob, routes, hidden_saved, w_out):
    experts, slot_count, slot_total = 32, 16, 512
    smem = pl.BlockSpec(memory_space=pltpu.SMEM)
    vmem = pl.BlockSpec(memory_space=pltpu.VMEM)
    params = pltpu.CompilerParams(vmem_limit_bytes=40 * 1024 * 1024)
    cost = pl.CostEstimate(
        flops=2 * 512 * 4096 * 192, bytes_accessed=6 * 1024 * 1024, transcendentals=0
    )
    gate_row = gate_prob.reshape(1, 256)
    outgoing, target = pl.pallas_call(
        place_kernel,
        out_shape=(
            jax.ShapeDtypeStruct((slot_total, 128), jnp.bfloat16),
            jax.ShapeDtypeStruct((1, 256), jnp.int32),
        ),
        in_specs=[vmem] * 3,
        out_specs=(vmem,) * 2,
        compiler_params=params,
        name="place",
    )(routes.reshape(1, 256), gate_row, grad_out)
    weight = w_out[0]
    saved = hidden_saved.reshape(slot_total, -1)
    replica = lax.axis_index("replica").astype(jnp.int32)
    at = jnp.stack([lax.rem(replica // 2, 4), lax.rem(replica, 2)])

    swap = pl.pallas_call(
        pack_kernel,
        out_shape=jax.ShapeDtypeStruct((4, 192, 1536), jnp.bfloat16),
        in_specs=[vmem] * 2,
        out_specs=vmem,
        compiler_params=params,
        cost_estimate=pl.CostEstimate(flops=0, bytes_accessed=4 * 1024 * 1024, transcendentals=0),
        name="pack",
    )(weight, saved)
    swapped = lax.all_to_all(
        swap, BOTH, 0, 0, tiled=True, axis_index_groups=groups("x")
    ).reshape(768, 1536)

    arrived = lax.all_to_all(
        outgoing.reshape(experts, slot_count, -1), "expert", 0, 0, tiled=True
    ).reshape(slot_total, -1)
    own = lax.all_gather(arrived, BOTH, axis=0, tiled=False, axis_index_groups=groups("hi"))
    other = lax.ppermute(own, "replica", [(i, i ^ 1) for i in range(32)])

    own_sums = pl.pallas_call(
        own_slots_kernel,
        out_shape=jax.ShapeDtypeStruct((1, slot_total), jnp.float32),
        in_specs=[smem, vmem, vmem],
        out_specs=vmem,
        compiler_params=params,
        cost_estimate=cost,
        name="own_slots",
    )(at, own, swapped)
    plane_sums = pl.pallas_call(
        slots_kernel,
        out_shape=jax.ShapeDtypeStruct((32, 1, 128), jnp.float32),
        in_specs=[smem] + [vmem] * 3,
        out_specs=vmem,
        compiler_params=params,
        cost_estimate=cost,
        name="slots",
    )(at, other, swapped, own_sums)
    from_plane = lax.all_to_all(
        plane_sums, BOTH, 0, 0, tiled=True, axis_index_groups=groups("y", "x", "core")
    )
    to_z = pl.pallas_call(
        turn_kernel,
        out_shape=jax.ShapeDtypeStruct((32, 1, 64), jnp.float32),
        in_specs=[vmem],
        out_specs=vmem,
        compiler_params=params,
        cost_estimate=pl.CostEstimate(flops=int(1e+10), bytes_accessed=1000, transcendentals=0),
        name="turn",
    )(from_plane)
    from_z = lax.all_to_all(
        to_z, BOTH, 0, 0, tiled=True, axis_index_groups=groups("hi", "lo")
    )
    going, _ = lax.optimization_barrier((own, plane_sums))
    own_rows = [own] + [
        lax.ppermute(
            going,
            "replica",
            [(i, i // 8 * 8 + (i % 8 // 2 + k) % 4 * 2 + i % 2) for i in range(32)],
        )
        for k in range(1, 4)
    ]
    other_rows = [other] + [
        lax.ppermute(rows, "replica", [(i, i ^ 1) for i in range(32)]) for rows in own_rows[1:]
    ]
    small = pl.CostEstimate(flops=1000, bytes_accessed=1000, transcendentals=0)
    hbm = pl.BlockSpec(memory_space=pl.ANY)
    sums, weight_part = pl.pallas_call(
        own_kernel,
        out_shape=(
            jax.ShapeDtypeStruct((192, slot_total), jnp.float32),
            jax.ShapeDtypeStruct(weight.shape, jnp.bfloat16),
        ),
        in_specs=[smem] + [vmem] * 7,
        out_specs=(vmem, hbm),
        scratch_shapes=[
            pltpu.VMEM((20, 192, 128), jnp.bfloat16), pltpu.SemaphoreType.DMA((20,))
        ],
        compiler_params=params,
        cost_estimate=small,
        name="own",
    )(at, weight, saved, *own_rows, other)
    from_z, sums, weight_part = lax.optimization_barrier((from_z, sums, weight_part))
    hidden_out, weight_out = pl.pallas_call(
        other_kernel,
        out_shape=(
            jax.ShapeDtypeStruct(saved.shape, jnp.bfloat16),
            jax.ShapeDtypeStruct(weight.shape, jnp.bfloat16),
        ),
        in_specs=[smem] + [vmem] * 6 + [hbm],
        out_specs=(vmem, hbm),
        input_output_aliases={7: 1},
        scratch_shapes=[
            pltpu.VMEM((12, 192, 128), jnp.bfloat16), pltpu.SemaphoreType.DMA((12,))
        ],
        compiler_params=params,
        cost_estimate=small,
        name="other",
    )(at, weight, saved, sums, *other_rows[1:], weight_part)
    grad_gate = pl.pallas_call(
        gate_kernel,
        out_shape=jax.ShapeDtypeStruct((1, 256), jnp.float32),
        in_specs=[vmem] * 3,
        out_specs=vmem,
        compiler_params=params,
        cost_estimate=pl.CostEstimate(flops=int(5e+09), bytes_accessed=1000, transcendentals=0),
        name="gate",
    )(from_z, target, gate_row)
    return (hidden_out.reshape(hidden_saved.shape), weight_out[None], grad_gate.reshape(256))


def solution(mesh):
    placed = (
        P("expert", "replica"),
        P("expert"),
        P("expert", None),
        P("expert", None, None, "replica"),
        P("expert", "replica", None),
    )
    return jax.shard_map(
        per_device,
        mesh=mesh,
        in_specs=placed,
        out_specs=(P("expert", None, None, "replica"), P("expert", "replica", None), P("expert")),
        check_vma=False,
    )
```

```python
import itertools

import jax
import jax.numpy as jnp
from jax import lax
from jax.experimental import pallas as pl
from jax.experimental.pallas import tpu as pltpu
from jax.sharding import PartitionSpec as P

SIZES = dict(y=4, lo=8, hi=4, x=4, core=2)
BOTH = ("expert", "replica")


def groups(*free):
    fixed = [name for name in SIZES if name not in free]
    out = []
    for held in itertools.product(*[range(SIZES[name]) for name in fixed]):
        at = dict(zip(fixed, held))
        group = []
        for moved in itertools.product(*[range(SIZES[name]) for name in free]):
            at.update(zip(free, moved))
            expert = at["y"] * SIZES["lo"] + at["lo"]
            replica = (at["hi"] * SIZES["x"] + at["x"]) * SIZES["core"] + at["core"]
            group.append(expert * 32 + replica)
        out.append(group)
    return out


def place_kernel(routes_ref, gate_ref, rows_ref, out_ref, target_ref):
    chosen = routes_ref[...]
    experts = lax.broadcasted_iota(jnp.int32, (32, 256), 0)
    onehot = jnp.where(experts == chosen, 1.0, 0.0)
    earlier = jnp.where(
        lax.broadcasted_iota(jnp.int32, (256, 256), 0)
        < lax.broadcasted_iota(jnp.int32, (256, 256), 1),
        1.0,
        0.0,
    ).astype(jnp.bfloat16)
    before = jnp.dot(onehot.astype(jnp.bfloat16), earlier, preferred_element_type=jnp.float32)
    position = jnp.sum(onehot * before, axis=0, keepdims=True).astype(jnp.int32)
    target = chosen * 16 + position
    target_ref[...] = target
    slots = lax.broadcasted_iota(jnp.int32, (512, 256), 0)
    placing = jnp.where(slots == target, gate_ref[...].astype(jnp.float32), 0.0)
    out_ref[...] = jnp.dot(
        placing.astype(jnp.bfloat16), rows_ref[...], preferred_element_type=jnp.float32
    ).astype(jnp.bfloat16)


def pack_kernel(w_ref, saved_ref, out_ref):
    saved = saved_ref[...].T
    for x in range(4):
        for hi in range(4):
            out_ref[x, :, hi * 256 : hi * 256 + 256] = w_ref[
                :, (hi * 4 + x) * 256 : (hi * 4 + x) * 256 + 256
            ]
        out_ref[x, :, 1024:] = saved


def product(left_ref, first_row, count, blocks):
    return lax.dot_general(
        jnp.concatenate(
            [left_ref[pl.ds(first_row, count), pl.ds(first, 128)] for _, first in blocks], axis=1
        ),
        jnp.concatenate([rows for rows, _ in blocks], axis=1),
        (((1,), (1,)), ((), ())),
        preferred_element_type=jnp.float32,
    )


def slot_sums(rows_ref, side, swap_ref):
    blocks = [
        (rows_ref[hi], pl.multiple_of(hi * 256 + side * 128, 128)) for hi in range(4)
    ]
    total = product(swap_ref, 0, 768, blocks)
    return jnp.sum(total * swap_ref[:, 1024:].astype(jnp.float32), axis=0, keepdims=True)


def own_slots_kernel(at_ref, rows_ref, swap_ref, out_ref):
    out_ref[...] = slot_sums(rows_ref, at_ref[1], swap_ref)


def slots_kernel(at_ref, rows_ref, swap_ref, own_ref, out_ref):
    sums = own_ref[...] + slot_sums(rows_ref, 1 - at_ref[1], swap_ref)
    for y in range(4):
        for i in range(8):
            out_ref[y * 8 + i] = sums[:, y * 128 : y * 128 + 128]


def turn_kernel(sums_ref, out_ref):
    rows = []
    for y in range(4):
        row = sums_ref[y * 8]
        for i in range(1, 8):
            row = row + sums_ref[y * 8 + i]
        rows.append(row)
    for lo in range(8):
        line = jnp.concatenate([row[:, lo * 16 : lo * 16 + 16] for row in rows], axis=1)
        for hi in range(4):
            out_ref[hi * 8 + lo] = line


def some_results(at_ref, w_ref, left, parts, weight_ref, held, sems):
    blocks, copies = [], []
    for row_ref, back, side in parts:
        source = lax.rem(at_ref[0] + 4 - back, 4)
        for hi in range(0, 4, 2):
            pair = [row_ref[hi], row_ref[hi + 1]]
            both = jnp.dot(
                left, jnp.concatenate(pair, axis=1), preferred_element_type=jnp.float32
            ).astype(jnp.bfloat16)
            for more, rows in enumerate(pair):
                first = pl.multiple_of(((hi + more) * 4 + source) * 256 + side * 128, 128)
                i = len(blocks)
                held[i] = both[:, more * 128 : more * 128 + 128]
                copy = pltpu.make_async_copy(
                    held.at[i], weight_ref.at[:, pl.ds(first, 128)], sems.at[i]
                )
                copy.start()
                blocks.append((rows, first))
                copies.append(copy)
    return product(w_ref, 0, 192, blocks), copies


def own_kernel(at_ref, w_ref, saved_ref, r0, r1, r2, r3, o0, sums_ref, weight_ref, held, sems):
    core = at_ref[1]
    parts = [(r0, 0, core), (o0, 0, 1 - core), (r1, 1, core), (r2, 2, core), (r3, 3, core)]
    left = saved_ref[...].T
    sums_ref[...], copies = some_results(at_ref, w_ref, left, parts, weight_ref, held, sems)
    for copy in copies:
        copy.wait()


def other_kernel(
    at_ref, w_ref, saved_ref, sums_ref, o1, o2, o3, started_ref, hidden_ref, weight_ref,
    held, sems, rows_in, sums_in, in_sems,
):
    arriving = [
        pltpu.make_async_copy(ref, rows_in.at[n], in_sems.at[n]) for n, ref in enumerate((o1, o2, o3))
    ] + [pltpu.make_async_copy(sums_ref, sums_in, in_sems.at[3])]
    for copy in arriving:
        copy.start()
    side, left = 1 - at_ref[1], saved_ref[...].T
    total, copies = None, []
    for n in range(3):
        arriving[n].wait()
        here = [(rows_in.at[n], n + 1, side)]
        term, more = some_results(
            at_ref, w_ref, left, here, weight_ref, held.at[pl.ds(n * 4, 4)], sems.at[pl.ds(n * 4, 4)]
        )
        total = term if total is None else total + term
        copies += more
    arriving[3].wait()
    hidden_ref[...] = (sums_in[...] + total).T.astype(jnp.bfloat16)
    for copy in copies:
        copy.wait()


def gate_kernel(sums_ref, target_ref, gate_ref, out_ref):
    total = sum(sums_ref[hi * 8 : hi * 8 + 8, 0, :64] for hi in range(4))
    columns = total.T
    target = target_ref[...]
    expert, slot = target // 16, target % 16
    place = expert // 8 * 16 + slot
    rows = lax.broadcasted_iota(jnp.int32, (64, 256), 0)
    found = jnp.zeros((64, 256), jnp.float32)
    for lo in range(8):
        hit = (rows == place) & (expert % 8 == lo)
        found = jnp.where(hit, columns[:, lo : lo + 1], found)
    out_ref[...] = jnp.sum(found, axis=0, keepdims=True) / gate_ref[...].astype(jnp.float32)


def per_device(grad_out, gate_prob, routes, hidden_saved, w_out):
    experts, slot_count, slot_total = 32, 16, 512
    smem = pl.BlockSpec(memory_space=pltpu.SMEM)
    vmem = pl.BlockSpec(memory_space=pltpu.VMEM)
    params = pltpu.CompilerParams(vmem_limit_bytes=40 * 1024 * 1024)
    cost = pl.CostEstimate(
        flops=2 * 512 * 4096 * 192, bytes_accessed=6 * 1024 * 1024, transcendentals=0
    )
    gate_row = gate_prob.reshape(1, 256)
    outgoing, target = pl.pallas_call(
        place_kernel,
        out_shape=(
            jax.ShapeDtypeStruct((slot_total, 128), jnp.bfloat16),
            jax.ShapeDtypeStruct((1, 256), jnp.int32),
        ),
        in_specs=[vmem] * 3,
        out_specs=(vmem,) * 2,
        compiler_params=params,
        name="place",
    )(routes.reshape(1, 256), gate_row, grad_out)
    weight = w_out[0]
    saved = hidden_saved.reshape(slot_total, -1)
    replica = lax.axis_index("replica").astype(jnp.int32)
    at = jnp.stack([lax.rem(replica // 2, 4), lax.rem(replica, 2)])

    swap = pl.pallas_call(
        pack_kernel,
        out_shape=jax.ShapeDtypeStruct((4, 192, 1536), jnp.bfloat16),
        in_specs=[vmem] * 2,
        out_specs=vmem,
        compiler_params=params,
        cost_estimate=pl.CostEstimate(flops=0, bytes_accessed=4 * 1024 * 1024, transcendentals=0),
        name="pack",
    )(weight, saved)
    swapped = lax.all_to_all(
        swap, BOTH, 0, 0, tiled=True, axis_index_groups=groups("x")
    ).reshape(768, 1536)

    arrived = lax.all_to_all(
        outgoing.reshape(experts, slot_count, -1), "expert", 0, 0, tiled=True
    ).reshape(slot_total, -1)
    own = lax.all_gather(arrived, BOTH, axis=0, tiled=False, axis_index_groups=groups("hi"))
    other = lax.ppermute(own, "replica", [(i, i ^ 1) for i in range(32)])

    own_sums = pl.pallas_call(
        own_slots_kernel,
        out_shape=jax.ShapeDtypeStruct((1, slot_total), jnp.float32),
        in_specs=[smem, vmem, vmem],
        out_specs=vmem,
        compiler_params=params,
        cost_estimate=cost,
        name="own_slots",
    )(at, own, swapped)
    plane_sums = pl.pallas_call(
        slots_kernel,
        out_shape=jax.ShapeDtypeStruct((32, 1, 128), jnp.float32),
        in_specs=[smem] + [vmem] * 3,
        out_specs=vmem,
        compiler_params=params,
        cost_estimate=cost,
        name="slots",
    )(at, other, swapped, own_sums)
    from_plane = lax.all_to_all(
        plane_sums, BOTH, 0, 0, tiled=True, axis_index_groups=groups("y", "x", "core")
    )
    to_z = pl.pallas_call(
        turn_kernel,
        out_shape=jax.ShapeDtypeStruct((32, 1, 64), jnp.float32),
        in_specs=[vmem],
        out_specs=vmem,
        compiler_params=params,
        cost_estimate=pl.CostEstimate(flops=int(1e+10), bytes_accessed=1000, transcendentals=0),
        name="turn",
    )(from_plane)
    from_z = lax.all_to_all(
        to_z, BOTH, 0, 0, tiled=True, axis_index_groups=groups("hi", "lo")
    )
    going, _ = lax.optimization_barrier((own, plane_sums))
    own_rows = [own] + [
        lax.ppermute(
            going,
            "replica",
            [(i, i // 8 * 8 + (i % 8 // 2 + k) % 4 * 2 + i % 2) for i in range(32)],
        )
        for k in range(1, 4)
    ]
    other_rows = [other] + [
        lax.ppermute(rows, "replica", [(i, i ^ 1) for i in range(32)]) for rows in own_rows[1:]
    ]
    small = pl.CostEstimate(flops=1000, bytes_accessed=1000, transcendentals=0)
    hbm = pl.BlockSpec(memory_space=pl.ANY)
    sums, weight_part = pl.pallas_call(
        own_kernel,
        out_shape=(
            jax.ShapeDtypeStruct((192, slot_total), jnp.float32),
            jax.ShapeDtypeStruct(weight.shape, jnp.bfloat16),
        ),
        in_specs=[smem] + [vmem] * 7,
        out_specs=(vmem, hbm),
        scratch_shapes=[
            pltpu.VMEM((20, 192, 128), jnp.bfloat16), pltpu.SemaphoreType.DMA((20,))
        ],
        compiler_params=params,
        cost_estimate=small,
        name="own",
    )(at, weight, saved, *own_rows, other)
    from_z, sums, weight_part = lax.optimization_barrier((from_z, sums, weight_part))
    hidden_out, weight_out = pl.pallas_call(
        other_kernel,
        out_shape=(
            jax.ShapeDtypeStruct(saved.shape, jnp.bfloat16),
            jax.ShapeDtypeStruct(weight.shape, jnp.bfloat16),
        ),
        in_specs=[smem] + [vmem] * 2 + [hbm] * 5,
        out_specs=(vmem, hbm),
        input_output_aliases={7: 1},
        scratch_shapes=[
            pltpu.VMEM((12, 192, 128), jnp.bfloat16),
            pltpu.SemaphoreType.DMA((12,)),
            pltpu.VMEM((3, 4, 512, 128), jnp.bfloat16),
            pltpu.VMEM((192, 512), jnp.float32),
            pltpu.SemaphoreType.DMA((4,)),
        ],
        compiler_params=params,
        cost_estimate=small,
        name="other",
    )(at, weight, saved, sums, *other_rows[1:], weight_part)
    grad_gate = pl.pallas_call(
        gate_kernel,
        out_shape=jax.ShapeDtypeStruct((1, 256), jnp.float32),
        in_specs=[vmem] * 3,
        out_specs=vmem,
        compiler_params=params,
        cost_estimate=pl.CostEstimate(flops=int(5e+09), bytes_accessed=1000, transcendentals=0),
        name="gate",
    )(from_z, target, gate_row)
    return (hidden_out.reshape(hidden_saved.shape), weight_out[None], grad_gate.reshape(256))


def solution(mesh):
    placed = (
        P("expert", "replica"),
        P("expert"),
        P("expert", None),
        P("expert", None, None, "replica"),
        P("expert", "replica", None),
    )
    return jax.shard_map(
        per_device,
        mesh=mesh,
        in_specs=placed,
        out_specs=(P("expert", None, None, "replica"), P("expert", "replica", None), P("expert")),
        check_vma=False,
    )
```

```python
import itertools

import jax
import jax.numpy as jnp
from jax import lax
from jax.experimental import pallas as pl
from jax.experimental.pallas import tpu as pltpu
from jax.sharding import PartitionSpec as P

SIZES = dict(y=4, lo=8, hi=4, x=4, core=2)
BOTH = ("expert", "replica")


def groups(*free):
    fixed = [name for name in SIZES if name not in free]
    out = []
    for held in itertools.product(*[range(SIZES[name]) for name in fixed]):
        at = dict(zip(fixed, held))
        group = []
        for moved in itertools.product(*[range(SIZES[name]) for name in free]):
            at.update(zip(free, moved))
            expert = at["y"] * SIZES["lo"] + at["lo"]
            replica = (at["hi"] * SIZES["x"] + at["x"]) * SIZES["core"] + at["core"]
            group.append(expert * 32 + replica)
        out.append(group)
    return out


def place_kernel(routes_ref, gate_ref, rows_ref, out_ref, target_ref):
    chosen = routes_ref[...]
    experts = lax.broadcasted_iota(jnp.int32, (32, 256), 0)
    onehot = jnp.where(experts == chosen, 1.0, 0.0)
    earlier = jnp.where(
        lax.broadcasted_iota(jnp.int32, (256, 256), 0)
        < lax.broadcasted_iota(jnp.int32, (256, 256), 1),
        1.0,
        0.0,
    ).astype(jnp.bfloat16)
    before = jnp.dot(onehot.astype(jnp.bfloat16), earlier, preferred_element_type=jnp.float32)
    position = jnp.sum(onehot * before, axis=0, keepdims=True).astype(jnp.int32)
    target = chosen * 16 + position
    target_ref[...] = target
    slots = lax.broadcasted_iota(jnp.int32, (512, 256), 0)
    placing = jnp.where(slots == target, gate_ref[...].astype(jnp.float32), 0.0)
    out_ref[...] = jnp.dot(
        placing.astype(jnp.bfloat16), rows_ref[...], preferred_element_type=jnp.float32
    ).astype(jnp.bfloat16)


def pack_kernel(w_ref, saved_ref, out_ref):
    saved = saved_ref[...].T
    for x in range(4):
        for hi in range(4):
            out_ref[x, :, hi * 256 : hi * 256 + 256] = w_ref[
                :, (hi * 4 + x) * 256 : (hi * 4 + x) * 256 + 256
            ]
        out_ref[x, :, 1024:] = saved


def product(left_ref, first_row, count, blocks):
    return lax.dot_general(
        jnp.concatenate(
            [left_ref[pl.ds(first_row, count), pl.ds(first, 128)] for _, first in blocks], axis=1
        ),
        jnp.concatenate([rows for rows, _ in blocks], axis=1),
        (((1,), (1,)), ((), ())),
        preferred_element_type=jnp.float32,
    )


def slot_sums(rows_ref, side, swap_ref):
    blocks = [
        (rows_ref[hi], pl.multiple_of(hi * 256 + side * 128, 128)) for hi in range(4)
    ]
    total = product(swap_ref, 0, 768, blocks)
    return jnp.sum(total * swap_ref[:, 1024:].astype(jnp.float32), axis=0, keepdims=True)


def own_slots_kernel(at_ref, rows_ref, swap_ref, out_ref):
    out_ref[...] = slot_sums(rows_ref, at_ref[1], swap_ref)


def slots_kernel(at_ref, rows_ref, swap_ref, own_ref, out_ref):
    sums = own_ref[...] + slot_sums(rows_ref, 1 - at_ref[1], swap_ref)
    for y in range(4):
        for i in range(8):
            out_ref[y * 8 + i] = sums[:, y * 128 : y * 128 + 128]


def turn_kernel(sums_ref, out_ref):
    rows = []
    for y in range(4):
        row = sums_ref[y * 8]
        for i in range(1, 8):
            row = row + sums_ref[y * 8 + i]
        rows.append(row)
    for lo in range(8):
        line = jnp.concatenate([row[:, lo * 16 : lo * 16 + 16] for row in rows], axis=1)
        for hi in range(4):
            out_ref[hi * 8 + lo] = line


def some_results(at_ref, w_ref, saved_ref, parts, weight_ref, held, sems):
    left = saved_ref[...].T
    blocks, copies = [], []
    for row_ref, back, side in parts:
        source = lax.rem(at_ref[0] + 4 - back, 4)
        for hi in range(0, 4, 2):
            pair = [row_ref[hi], row_ref[hi + 1]]
            both = jnp.dot(
                left, jnp.concatenate(pair, axis=1), preferred_element_type=jnp.float32
            ).astype(jnp.bfloat16)
            for more, rows in enumerate(pair):
                first = pl.multiple_of(((hi + more) * 4 + source) * 256 + side * 128, 128)
                i = len(blocks)
                held[i] = both[:, more * 128 : more * 128 + 128]
                copy = pltpu.make_async_copy(
                    held.at[i], weight_ref.at[:, pl.ds(first, 128)], sems.at[i]
                )
                copy.start()
                blocks.append((rows, first))
                copies.append(copy)
    return product(w_ref, 0, 192, blocks), copies


def own_kernel(at_ref, w_ref, saved_ref, r3, r2, r1, r0, o0, sums_ref, weight_ref, held, sems):
    core = at_ref[1]
    parts = [(r0, 0, core), (o0, 0, 1 - core), (r1, 1, core), (r2, 2, core), (r3, 3, core)]
    sums_ref[...], copies = some_results(at_ref, w_ref, saved_ref, parts, weight_ref, held, sems)
    for copy in copies:
        copy.wait()


def other_kernel(
    at_ref, w_ref, saved_ref, sums_ref, o1, o2, o3, started_ref, hidden_ref, weight_ref, held, sems
):
    side = 1 - at_ref[1]
    parts = [(o1, 1, side), (o2, 2, side), (o3, 3, side)]
    total, copies = some_results(at_ref, w_ref, saved_ref, parts, weight_ref, held, sems)
    hidden_ref[...] = (sums_ref[...] + total).T.astype(jnp.bfloat16)
    for copy in copies:
        copy.wait()


def gate_kernel(sums_ref, target_ref, gate_ref, out_ref):
    total = sum(sums_ref[hi * 8 : hi * 8 + 8, 0, :64] for hi in range(4))
    columns = total.T
    target = target_ref[...]
    expert, slot = target // 16, target % 16
    place = expert // 8 * 16 + slot
    rows = lax.broadcasted_iota(jnp.int32, (64, 256), 0)
    found = jnp.zeros((64, 256), jnp.float32)
    for lo in range(8):
        hit = (rows == place) & (expert % 8 == lo)
        found = jnp.where(hit, columns[:, lo : lo + 1], found)
    out_ref[...] = jnp.sum(found, axis=0, keepdims=True) / gate_ref[...].astype(jnp.float32)


def per_device(grad_out, gate_prob, routes, hidden_saved, w_out):
    experts, slot_count, slot_total = 32, 16, 512
    smem = pl.BlockSpec(memory_space=pltpu.SMEM)
    vmem = pl.BlockSpec(memory_space=pltpu.VMEM)
    params = pltpu.CompilerParams(vmem_limit_bytes=40 * 1024 * 1024)
    cost = pl.CostEstimate(
        flops=2 * 512 * 4096 * 192, bytes_accessed=6 * 1024 * 1024, transcendentals=0
    )
    gate_row = gate_prob.reshape(1, 256)
    outgoing, target = pl.pallas_call(
        place_kernel,
        out_shape=(
            jax.ShapeDtypeStruct((slot_total, 128), jnp.bfloat16),
            jax.ShapeDtypeStruct((1, 256), jnp.int32),
        ),
        in_specs=[vmem] * 3,
        out_specs=(vmem,) * 2,
        compiler_params=params,
        name="place",
    )(routes.reshape(1, 256), gate_row, grad_out)
    weight = w_out[0]
    saved = hidden_saved.reshape(slot_total, -1)
    replica = lax.axis_index("replica").astype(jnp.int32)
    at = jnp.stack([lax.rem(replica // 2, 4), lax.rem(replica, 2)])

    swap = pl.pallas_call(
        pack_kernel,
        out_shape=jax.ShapeDtypeStruct((4, 192, 1536), jnp.bfloat16),
        in_specs=[vmem] * 2,
        out_specs=vmem,
        compiler_params=params,
        cost_estimate=pl.CostEstimate(flops=0, bytes_accessed=4 * 1024 * 1024, transcendentals=0),
        name="pack",
    )(weight, saved)
    swapped = lax.all_to_all(
        swap, BOTH, 0, 0, tiled=True, axis_index_groups=groups("x")
    ).reshape(768, 1536)

    arrived = lax.all_to_all(
        outgoing.reshape(experts, slot_count, -1), "expert", 0, 0, tiled=True
    ).reshape(slot_total, -1)
    own = lax.all_gather(arrived, BOTH, axis=0, tiled=False, axis_index_groups=groups("hi"))
    other = lax.ppermute(own, "replica", [(i, i ^ 1) for i in range(32)])

    own_sums = pl.pallas_call(
        own_slots_kernel,
        out_shape=jax.ShapeDtypeStruct((1, slot_total), jnp.float32),
        in_specs=[smem, vmem, vmem],
        out_specs=vmem,
        compiler_params=params,
        cost_estimate=cost,
        name="own_slots",
    )(at, own, swapped)
    plane_sums = pl.pallas_call(
        slots_kernel,
        out_shape=jax.ShapeDtypeStruct((32, 1, 128), jnp.float32),
        in_specs=[smem] + [vmem] * 3,
        out_specs=vmem,
        compiler_params=params,
        cost_estimate=cost,
        name="slots",
    )(at, other, swapped, own_sums)
    from_plane = lax.all_to_all(
        plane_sums, BOTH, 0, 0, tiled=True, axis_index_groups=groups("y", "x", "core")
    )
    to_z = pl.pallas_call(
        turn_kernel,
        out_shape=jax.ShapeDtypeStruct((32, 1, 64), jnp.float32),
        in_specs=[vmem],
        out_specs=vmem,
        compiler_params=params,
        cost_estimate=pl.CostEstimate(flops=int(1e+10), bytes_accessed=1000, transcendentals=0),
        name="turn",
    )(from_plane)
    from_z = lax.all_to_all(
        to_z, BOTH, 0, 0, tiled=True, axis_index_groups=groups("hi", "lo")
    )
    going, _ = lax.optimization_barrier((own, plane_sums))
    own_rows = [own] + [
        lax.ppermute(
            going,
            "replica",
            [(i, i // 8 * 8 + (i % 8 // 2 + k) % 4 * 2 + i % 2) for i in range(32)],
        )
        for k in range(1, 4)
    ]
    other_rows = [other] + [
        lax.ppermute(rows, "replica", [(i, i ^ 1) for i in range(32)]) for rows in own_rows[1:]
    ]
    small = pl.CostEstimate(flops=1000, bytes_accessed=1000, transcendentals=0)
    hbm = pl.BlockSpec(memory_space=pl.ANY)
    sums, weight_part = pl.pallas_call(
        own_kernel,
        out_shape=(
            jax.ShapeDtypeStruct((192, slot_total), jnp.float32),
            jax.ShapeDtypeStruct(weight.shape, jnp.bfloat16),
        ),
        in_specs=[smem] + [vmem] * 7,
        out_specs=(vmem, hbm),
        scratch_shapes=[
            pltpu.VMEM((20, 192, 128), jnp.bfloat16), pltpu.SemaphoreType.DMA((20,))
        ],
        compiler_params=params,
        cost_estimate=small,
        name="own",
    )(at, weight, saved, *own_rows[::-1], other)
    from_z, sums, weight_part = lax.optimization_barrier((from_z, sums, weight_part))
    hidden_out, weight_out = pl.pallas_call(
        other_kernel,
        out_shape=(
            jax.ShapeDtypeStruct(saved.shape, jnp.bfloat16),
            jax.ShapeDtypeStruct(weight.shape, jnp.bfloat16),
        ),
        in_specs=[smem] + [vmem] * 6 + [hbm],
        out_specs=(vmem, hbm),
        input_output_aliases={7: 1},
        scratch_shapes=[
            pltpu.VMEM((12, 192, 128), jnp.bfloat16), pltpu.SemaphoreType.DMA((12,))
        ],
        compiler_params=params,
        cost_estimate=small,
        name="other",
    )(at, weight, saved, sums, *other_rows[1:], weight_part)
    grad_gate = pl.pallas_call(
        gate_kernel,
        out_shape=jax.ShapeDtypeStruct((1, 256), jnp.float32),
        in_specs=[vmem] * 3,
        out_specs=vmem,
        compiler_params=params,
        cost_estimate=pl.CostEstimate(flops=int(5e+09), bytes_accessed=1000, transcendentals=0),
        name="gate",
    )(from_z, target, gate_row)
    return (hidden_out.reshape(hidden_saved.shape), weight_out[None], grad_gate.reshape(256))


def solution(mesh):
    placed = (
        P("expert", "replica"),
        P("expert"),
        P("expert", None),
        P("expert", None, None, "replica"),
        P("expert", "replica", None),
    )
    return jax.shard_map(
        per_device,
        mesh=mesh,
        in_specs=placed,
        out_specs=(P("expert", None, None, "replica"), P("expert", "replica", None), P("expert")),
        check_vma=False,
    )
```
